32 devices in a mesh: rad: 8 (over y, x, core), azi: 4 (over z).
Axes of the slice: x: 2, y: 2, z: 4, core: 2. Of those that a mesh axis runs over, the one named last changes fastest.
Arguments:
- state: float32 [5, 4, 128, 512], P(None, None, 'rad', 'azi'), may hold values from -6 to 6
- shifts: int32 [128], replicated, may hold values from 0 to 511
- spin: float32 [128], replicated, may hold values from 0.2 to 1
- drift: float32 [128], replicated, may hold values from -1.5 to 1.5
- stiffness: float32 [4, 128], replicated, may hold values from 0.5 to 2
Outputs:
- evolved: float32 [5, 4, 128, 512], P(None, None, 'rad', 'azi')
The draws below stay inside these ranges and needn't reach their ends.
All inputs are finite; a program needn't handle non-finite values.
Results may differ from the reference program's by a relative error of at most 0.00002.
Values sent between devices are 32-bit elements; how exact they have to be, the bound alone decides.
A program may use at most 64 MiB of HBM per device.

```python
import math
import jax
import jax.numpy as jnp

NV = 4
STEPS = 2
NR = 128
NA = 512


def plant(array, own_key, smallest, top_value):
    longest = array.shape.index(max(array.shape))
    spots = []
    for shift in (0, 1):
        where = [jax.random.randint(jax.random.fold_in(own_key, axis), (), 0, length) for axis, length in enumerate(array.shape)]
        where[longest] = (where[longest] + shift) % array.shape[longest]
        spots.append(tuple(where))
    return array.at[spots[0]].set(smallest).at[spots[1]].set(top_value)


def level_of(stream_key, shape, pieces, least, top_value):
    level = 1.0
    for dim, shards_of in pieces:
        heights = jax.random.uniform(jax.random.fold_in(jax.random.fold_in(stream_key, 6), dim), (shards_of,), jnp.float32, least / len(pieces), top_value / len(pieces))
        level = level * jnp.repeat(jnp.exp(heights), shape[dim] // shards_of).reshape((-1,) + (1,) * (len(shape) - 1 - dim))
    return level


def normal_values(own_key, extent, spread, reach, shards=(), kind=jnp.bfloat16):
    values = spread * jax.random.normal(own_key, extent, jnp.float32)
    if shards:
        values = values * level_of(own_key, extent, shards, -0.22, 0.18)
    return jnp.clip(values, -reach, reach).astype(kind)


def setup_inputs(seed: int = 0) -> dict:
    keys = jax.random.split(jax.random.key(seed), 6)
    state = normal_values(keys[0], (5, NV, NR, NA), 1.0, 6.0, ((2, 8), (3, 4)), jnp.float32)
    shifts = plant(jax.random.randint(keys[1], (NR,), 0, NA), jax.random.fold_in(keys[1], 1), 0, NA - 1).astype(jnp.int32)
    spin = jnp.clip(jnp.exp(jax.random.uniform(keys[2], (NR,), jnp.float32, math.log(0.2), math.log(1.0))), 0.2, 1.0)
    drift = jnp.clip(jax.random.uniform(keys[3], (NR,), jnp.float32, -1.5, 1.5), -1.5, 1.5)
    stiffness = jnp.clip(jnp.exp(jax.random.uniform(keys[4], (NV, NR), jnp.float32, math.log(0.5), math.log(2.0))), 0.5, 2.0)
    return dict(state=state, shifts=shifts, spin=spin, drift=drift, stiffness=stiffness)


time_step = 0.15
diffuse = 0.05


def tendency(extended, stiff_rows, spin_rows, drift_rows):
    centre_cells = extended[:, :, 1:-1, 1:-1]
    upper_row = extended[:, :, 2:, 1:-1]
    lower_row = extended[:, :, :-2, 1:-1]
    ahead_cell = extended[:, :, 1:-1, 2:]
    behind_cell = extended[:, :, 1:-1, :-2]
    rad_slope = 0.5 * (upper_row - lower_row)
    azi_slope = 0.5 * (ahead_cell - behind_cell)
    laplace_sum = upper_row + lower_row + ahead_cell + behind_cell - 4.0 * centre_cells
    vertical_pad = jnp.pad(centre_cells[3:5], ((0, 0), (1, 1), (0, 0), (0, 0)))
    ver_slope = 0.5 * (vertical_pad[:, 2:] - vertical_pad[:, :-2])
    spin_col = spin_rows[:, None]
    drift_col = drift_rows[:, None]
    divergence = rad_slope[1] + azi_slope[2] + ver_slope[0]
    coupled = jnp.stack([
        -divergence,
        2.0 * spin_col * centre_cells[2] - rad_slope[4],
        -0.5 * spin_col * centre_cells[1] - azi_slope[4],
        -ver_slope[1],
        -stiff_rows[:, :, None] * divergence,
    ])
    return coupled - drift_col * azi_slope + diffuse * laplace_sum


def extend_grid(field):
    padded = jnp.pad(field, ((0, 0), (0, 0), (1, 1), (0, 0)))
    return jnp.concatenate([padded[..., -1:], padded, padded[..., :1]], axis=3)


def rotate_rows(field, shifts):
    total = field.shape[3]
    source_index = (jnp.arange(total, dtype=jnp.int32)[None, :] - shifts[:, None]) % total
    merged = field.reshape(-1, field.shape[2], total)
    moved = jax.vmap(lambda plane: jnp.take_along_axis(plane, source_index, axis=1))(merged)
    return moved.reshape(field.shape)


def reference(state, shifts, spin, drift, stiffness):
    current = state
    for step_index in range(STEPS):
        first = current + time_step * tendency(extend_grid(current), stiffness, spin, drift)
        second = 0.75 * current + 0.25 * (first + time_step * tendency(extend_grid(first), stiffness, spin, drift))
        sectioned = current / 3.0 + (2.0 / 3.0) * (second + time_step * tendency(extend_grid(second), stiffness, spin, drift))
        current = rotate_rows(sectioned, shifts)
    return current
```

```python
import functools

import jax
import jax.numpy as jnp
from jax import lax
from jax.experimental import pallas as pl
from jax.experimental.pallas import tpu as pltpu
from jax.sharding import PartitionSpec as P

MESH = pl.DeviceIdType.MESH
STEPS = 2
HALO = 8
LANES = 128
LEVELS = 4
time_step = 0.15
diffuse = 0.05


def gather_kernel(nrad, nazi, x_ref, ext_ref, zeros, own_sem, z_send, z_recv, h_send, h_recv, edge_sem):
    rad, azi = lax.axis_index("rad"), lax.axis_index("azi")
    rows = x_ref.shape[1]
    has_low, has_high = rad > 0, rad < nrad - 1

    barrier = pltpu.get_barrier_semaphore()
    for d in range(1, nazi):
        pl.semaphore_signal(barrier, inc=1, device_id=(rad, lax.rem(azi + d, nazi)), device_id_type=MESH)

    @pl.when(has_low)
    def _():
        pl.semaphore_signal(barrier, inc=1, device_id=(rad - 1, azi), device_id_type=MESH)

    @pl.when(has_high)
    def _():
        pl.semaphore_signal(barrier, inc=1, device_id=(rad + 1, azi), device_id_type=MESH)

    own = pltpu.make_async_copy(x_ref, ext_ref.at[azi, :, pl.ds(HALO, rows)], own_sem)
    own.start()
    zeros[...] = jnp.zeros_like(zeros)
    pl.semaphore_wait(barrier, nazi - 1 + has_low.astype(jnp.int32) + has_high.astype(jnp.int32))

    def along(d):
        return pltpu.make_async_remote_copy(
            src_ref=x_ref,
            dst_ref=ext_ref.at[azi, :, pl.ds(HALO, rows)],
            send_sem=z_send.at[d],
            recv_sem=z_recv.at[d],
            device_id=(rad, lax.rem(azi + d, nazi)),
            device_id_type=MESH,
        )

    def to_low(d):
        block = lax.rem(azi + nazi - d, nazi)
        src = x_ref.at[:, pl.ds(0, HALO)] if d == 0 else ext_ref.at[block, :, pl.ds(HALO, HALO)]
        return pltpu.make_async_remote_copy(
            src_ref=src,
            dst_ref=ext_ref.at[block, :, pl.ds(HALO + rows, HALO)],
            send_sem=h_send.at[0, d],
            recv_sem=h_recv.at[0, d],
            device_id=(rad - 1, azi),
            device_id_type=MESH,
        )

    def to_high(d):
        block = lax.rem(azi + nazi - d, nazi)
        src = x_ref.at[:, pl.ds(rows - HALO, HALO)] if d == 0 else ext_ref.at[block, :, pl.ds(rows, HALO)]
        return pltpu.make_async_remote_copy(
            src_ref=src,
            dst_ref=ext_ref.at[block, :, pl.ds(0, HALO)],
            send_sem=h_send.at[1, d],
            recv_sem=h_recv.at[1, d],
            device_id=(rad + 1, azi),
            device_id_type=MESH,
        )

    def edge(b, side):
        start = 0 if side == 0 else HALO + rows
        return pltpu.make_async_copy(zeros, ext_ref.at[b, :, pl.ds(start, HALO)], edge_sem.at[side, b])

    order = sorted(range(1, nazi), key=lambda d: min(d, nazi - d))
    for d in order:
        along(d).start()
    for d in [0] + order:
        if d:
            along(d).wait_recv()

        @pl.when(has_low)
        def _():
            to_low(d).start()

        @pl.when(has_high)
        def _():
            to_high(d).start()

    @pl.when(jnp.logical_not(has_low))
    def _():
        for b in range(nazi):
            edge(b, 0).start()
        for b in range(nazi):
            edge(b, 0).wait()

    @pl.when(jnp.logical_not(has_high))
    def _():
        for b in range(nazi):
            edge(b, 1).start()
        for b in range(nazi):
            edge(b, 1).wait()

    own.wait()
    for d in order:
        along(d).wait_send()

    @pl.when(has_low)
    def _():
        for d in range(nazi):
            to_low(d).wait_send()
            to_high(d).wait_recv()

    @pl.when(has_high)
    def _():
        for d in range(nazi):
            to_high(d).wait_send()
            to_low(d).wait_recv()


def gathered(x, nrad, nazi):
    planes, rows, cells = x.shape
    return pl.pallas_call(
        functools.partial(gather_kernel, nrad, nazi),
        out_shape=jax.ShapeDtypeStruct((nazi, planes, rows + 2 * HALO, cells), jnp.float32),
        in_specs=[pl.BlockSpec(memory_space=pl.ANY)],
        out_specs=pl.BlockSpec(memory_space=pl.ANY),
        scratch_shapes=[
            pltpu.VMEM((planes, HALO, cells), jnp.float32),
            pltpu.SemaphoreType.DMA,
            pltpu.SemaphoreType.DMA((nazi,)),
            pltpu.SemaphoreType.DMA((nazi,)),
            pltpu.SemaphoreType.DMA((2, nazi)),
            pltpu.SemaphoreType.DMA((2, nazi)),
            pltpu.SemaphoreType.DMA((2, nazi)),
        ],
        compiler_params=pltpu.CompilerParams(collective_id=0, has_side_effects=True),
    )(x)


def starts_for(first, last):
    starts = list(range(first, last - 6, 8))
    if starts[-1] + 7 < last:
        starts.append(last - 7)
    return starts


def stage(src, base, dst, coef, first, last, old, new):
    nazi = src.shape[0]
    lane = lax.broadcasted_iota(jnp.int32, (8, LANES), 1)
    at_end, at_start = lane == LANES - 1, lane == 0

    def body(j, carry):
        before = lax.rem(j + nazi - 1, nazi)
        after = lax.rem(j + 1, nazi)
        for s in starts_for(first, last):
            c0, d, ga, gb, h, s2, s5 = (coef[i, s : s + 8, :] for i in range(7))
            stiff = [coef[7 + k, s : s + 8, :] for k in range(LEVELS)]

            def cell(f, k):
                return src[j, f * LEVELS + k, s : s + 8, :]

            def around(f, k):
                p = f * LEVELS + k
                c = src[j, p, s : s + 8, :]
                up, lo = src[j, p, s + 1 : s + 9, :], src[j, p, s - 1 : s + 7, :]
                be = pltpu.roll(jnp.where(at_end, src[before, p, s : s + 8, :], c), 1, 1)
                ah = pltpu.roll(jnp.where(at_start, src[after, p, s : s + 8, :], c), LANES - 1, 1)
                return c, up, lo, ah, be

            def rest(parts):
                c, up, lo, ah, be = parts
                return c0 * c + d * (up + lo) + (ga * ah + gb * be)

            def vertical(f, k):
                if k == 0:
                    return cell(f, 1)
                if k == LEVELS - 1:
                    return -cell(f, k - 1)
                return cell(f, k + 1) - cell(f, k - 1)

            for k in range(LEVELS):
                rho, u, v, w, p = (around(f, k) for f in range(5))
                div = (u[1] - u[2]) + (v[3] - v[4]) + vertical(3, k)
                results = (
                    rest(rho) - h * div,
                    rest(u) + s2 * v[0] - h * (p[1] - p[2]),
                    rest(v) - s5 * u[0] - h * (p[3] - p[4]),
                    rest(w) - h * vertical(4, k),
                    rest(p) - stiff[k] * div,
                )
                for f, result in enumerate(results):
                    plane = f * LEVELS + k
                    if base is not None:
                        result = old * base[j, plane, s : s + 8, :] + new * result
                    dst[j, plane, s : s + 8, :] = result
        return carry

    lax.fori_loop(0, nazi, body, 0)


def compute_kernel(azi_ref, ext_ref, coef_ref, out_ref, one, two, three):
    nazi, planes, rows, cells = ext_ref.shape
    reach = HALO
    low, high = HALO, rows - HALO - 1
    lane = lax.broadcasted_iota(jnp.int32, (8, LANES), 1)

    def section(current, margin, x, y, z):
        stage(current, None, x, coef_ref, low - margin - 2, high + margin + 2, 0.0, 1.0)
        stage(x, current, y, coef_ref, low - margin - 1, high + margin + 1, 0.75, 0.25)
        stage(y, current, z, coef_ref, low - margin, high + margin, 1.0 / 3.0, 2.0 / 3.0)

    def amounts(s):
        shift = coef_ref[11, s : s + 8, :].astype(jnp.int32)
        return shift // LANES, shift % LANES

    def rotate(here, behind, offsets):
        mixed = jnp.where(lane >= LANES - offsets, behind, here)
        return jnp.take_along_axis(mixed, lax.rem(lane - offsets + LANES, LANES), axis=1)

    section(ext_ref, 3, one, two, three)
    for s in starts_for(low - 3, high + 3):
        hops, offsets = amounts(s)

        def shifted(p, carry):
            blocks = [three[b, p, s : s + 8, :] for b in range(nazi)]
            blocks = [rotate(blocks[b], blocks[b - 1], offsets) for b in range(nazi)]
            for bit in range(nazi.bit_length() - 1):
                taken = (hops // (1 << bit)) % 2 == 1
                blocks = [jnp.where(taken, blocks[b - (1 << bit)], blocks[b]) for b in range(nazi)]
            for b in range(nazi):
                one[b, p, s : s + 8, :] = blocks[b]
            return carry

        lax.fori_loop(0, planes, shifted, 0)

    stage(one, None, two, coef_ref, low - 2, high + 2, 0.0, 1.0)
    stage(two, one, three, coef_ref, low - 1, high + 1, 0.75, 0.25)
    stage(three, one, two, coef_ref, low, high, 1.0 / 3.0, 2.0 / 3.0)
    azi = azi_ref[0]
    for s in starts_for(low, high):
        hops, offsets = amounts(s)
        source = lax.rem(azi - hops + nazi, nazi)

        def final(p, carry):
            blocks = [two[b, p, s : s + 8, :] for b in range(nazi)]
            here, behind = blocks[0], blocks[-1]
            for b in range(1, nazi):
                here = jnp.where(source == b, blocks[b], here)
                behind = jnp.where(source == b, blocks[b - 1], behind)
            out_ref[p, s - HALO : s, :] = rotate(here, behind, offsets)
            return carry

        lax.fori_loop(0, planes, final, 0)


def on_device(state, shifts, spin, drift, stiffness):
    fields, levels, rows, cells = state.shape
    planes = fields * levels
    nrad, nazi = lax.axis_size("rad"), lax.axis_size("azi")
    wide = rows + 2 * HALO
    flat = state.reshape(planes, rows, cells)

    c = time_step * diffuse
    half = 0.5 * time_step
    unit = jnp.ones_like(spin)
    table = jnp.concatenate(
        [
            jnp.stack(
                [
                    (1.0 - 4.0 * c) * unit,
                    c * unit,
                    c - half * drift,
                    c + half * drift,
                    half * unit,
                    2.0 * time_step * spin,
                    half * spin,
                ]
            ),
            half * stiffness,
            shifts.astype(jnp.float32)[None],
        ]
    )
    padded = jnp.pad(table, ((0, 0), (HALO, HALO)))
    mine = lax.dynamic_slice_in_dim(padded, lax.axis_index("rad") * rows, wide, axis=1)
    coef = jnp.broadcast_to(mine[:, :, None], (table.shape[0], wide, cells))
    place = lax.axis_index("azi").astype(jnp.int32).reshape(1)

    ext = gathered(flat, nrad, nazi)
    whole = pltpu.VMEM(ext.shape, jnp.float32)
    out = pl.pallas_call(
        compute_kernel,
        out_shape=jax.ShapeDtypeStruct(flat.shape, jnp.float32),
        in_specs=[
            pl.BlockSpec(memory_space=pltpu.SMEM),
            pl.BlockSpec(memory_space=pltpu.VMEM),
            pl.BlockSpec(memory_space=pltpu.VMEM),
        ],
        out_specs=pl.BlockSpec(memory_space=pltpu.VMEM),
        scratch_shapes=[whole, whole, whole],
        compiler_params=pltpu.CompilerParams(vmem_limit_bytes=40 * 2**20),
    )(place, ext, coef)
    return out.reshape(state.shape)


def solution(mesh):
    in_specs = (P(None, None, "rad", "azi"), P(), P(), P(), P())
    out_specs = P(None, None, "rad", "azi")
    return jax.shard_map(
        on_device, mesh=mesh, in_specs=in_specs, out_specs=out_specs, check_vma=False
    )
```

```python
import functools

import jax
import jax.numpy as jnp
from jax import lax
from jax.experimental import pallas as pl
from jax.experimental.pallas import tpu as pltpu
from jax.sharding import PartitionSpec as P

MESH = pl.DeviceIdType.MESH
STEPS = 2
HALO = 8
OWN = 16
LANES = 128
LEVELS = 4
time_step = 0.15
diffuse = 0.05


def gather_kernel(nrad, nazi, x_ref, ext_ref, zeros, own_sem, z_send, z_recv, h_send, h_recv, edge_sem):
    rad, azi = lax.axis_index("rad"), lax.axis_index("azi")
    rows = x_ref.shape[1]
    has_low, has_high = rad > 0, rad < nrad - 1

    has_left, has_right = azi > 0, azi < nazi - 1
    neighbours = ((has_left, rad, azi - 1), (has_right, rad, azi + 1), (has_low, rad - 1, azi), (has_high, rad + 1, azi))

    barrier = pltpu.get_barrier_semaphore()
    expected = 0
    for present, to_rad, to_azi in neighbours:
        expected = expected + present.astype(jnp.int32)

        @pl.when(present)
        def _():
            pl.semaphore_signal(barrier, inc=1, device_id=(to_rad, to_azi), device_id_type=MESH)

    own = pltpu.make_async_copy(x_ref, ext_ref.at[azi, :, pl.ds(OWN, rows)], own_sem)
    own.start()
    zeros[...] = jnp.zeros_like(zeros)
    pl.semaphore_wait(barrier, expected)

    def along(side, t):
        block = azi - t if side == 0 else azi + t
        src = x_ref if t == 0 else ext_ref.at[block, :, pl.ds(OWN, rows)]
        return pltpu.make_async_remote_copy(
            src_ref=src,
            dst_ref=ext_ref.at[block, :, pl.ds(OWN, rows)],
            send_sem=z_send.at[side, t],
            recv_sem=z_recv.at[side, t],
            device_id=(rad, azi + 1 if side == 0 else azi - 1),
            device_id_type=MESH,
        )

    def sends(side, t):
        if side == 0:
            return jnp.logical_and(azi - t >= 0, has_right)
        return jnp.logical_and(azi + t < nazi, has_left)

    def arrives(side, t):
        return azi - 1 - t >= 0 if side == 0 else azi + 1 + t < nazi

    def arrived(side, t):
        block = azi - 1 - t if side == 0 else azi + 1 + t
        return pltpu.make_async_remote_copy(
            src_ref=x_ref,
            dst_ref=ext_ref.at[block, :, pl.ds(OWN, rows)],
            send_sem=z_send.at[side, t],
            recv_sem=z_recv.at[side, t],
            device_id=(rad, azi + 1 if side == 0 else azi - 1),
            device_id_type=MESH,
        )

    def radial(to, block, own_block):
        if to == 0:
            start, there = 0, OWN + rows
        else:
            start, there = rows - HALO, OWN - HALO
        src = x_ref.at[:, pl.ds(start, HALO)] if own_block else ext_ref.at[block, :, pl.ds(OWN + start, HALO)]
        return pltpu.make_async_remote_copy(
            src_ref=src,
            dst_ref=ext_ref.at[block, :, pl.ds(there, HALO)],
            send_sem=h_send.at[to, block],
            recv_sem=h_recv.at[to, block],
            device_id=(rad - 1 if to == 0 else rad + 1, azi),
            device_id_type=MESH,
        )

    def pass_on(block, own_block=False):
        @pl.when(has_low)
        def _():
            radial(0, block, own_block).start()

        @pl.when(has_high)
        def _():
            radial(1, block, own_block).start()

    def edge(b, side):
        start = OWN - HALO if side == 0 else OWN + rows
        return pltpu.make_async_copy(zeros, ext_ref.at[b, :, pl.ds(start, HALO)], edge_sem.at[side, b])

    for side in range(2):

        @pl.when(sends(side, 0))
        def _():
            along(side, 0).start()

    pass_on(azi, True)
    for side, missing in enumerate((has_low, has_high)):

        @pl.when(jnp.logical_not(missing))
        def _():
            for b in range(nazi):
                edge(b, side).start()

    for t in range(nazi - 1):
        for side in range(2):

            @pl.when(arrives(side, t))
            def _():
                arrived(side, t).wait_recv()

                @pl.when(sends(side, t + 1))
                def _():
                    along(side, t + 1).start()

                pass_on(azi - 1 - t if side == 0 else azi + 1 + t)

    for side, missing in enumerate((has_low, has_high)):

        @pl.when(jnp.logical_not(missing))
        def _():
            for b in range(nazi):
                edge(b, side).wait()

    own.wait()
    for t in range(nazi - 1):
        for side in range(2):

            @pl.when(sends(side, t))
            def _():
                along(side, t).wait_send()

    @pl.when(has_low)
    def _():
        for b in range(nazi):
            radial(0, b, False).wait_send()
            radial(1, b, False).wait_recv()

    @pl.when(has_high)
    def _():
        for b in range(nazi):
            radial(1, b, False).wait_send()
            radial(0, b, False).wait_recv()


def gathered(x, nrad, nazi):
    planes, rows, cells = x.shape
    return pl.pallas_call(
        functools.partial(gather_kernel, nrad, nazi),
        out_shape=jax.ShapeDtypeStruct((nazi, planes, rows + 2 * OWN, cells), jnp.float32),
        in_specs=[pl.BlockSpec(memory_space=pl.ANY)],
        out_specs=pl.BlockSpec(memory_space=pl.ANY),
        scratch_shapes=[
            pltpu.VMEM((planes, HALO, cells), jnp.float32),
            pltpu.SemaphoreType.DMA,
            pltpu.SemaphoreType.DMA((2, nazi)),
            pltpu.SemaphoreType.DMA((2, nazi)),
            pltpu.SemaphoreType.DMA((2, nazi)),
            pltpu.SemaphoreType.DMA((2, nazi)),
            pltpu.SemaphoreType.DMA((2, nazi)),
        ],
        compiler_params=pltpu.CompilerParams(collective_id=0, has_side_effects=True),
    )(x)


def stage(src, base, dst, coef, tiles, old, new):
    nazi = src.shape[0]
    lane = lax.broadcasted_iota(jnp.int32, (8, LANES), 1)
    at_end, at_start = lane == LANES - 1, lane == 0

    def body(j, carry):
        before = lax.rem(j + nazi - 1, nazi)
        after = lax.rem(j + 1, nazi)
        for s in tiles:
            c0, d, ga, gb, h, s2, s5 = (coef[i, s : s + 8, :] for i in range(7))
            stiff = [coef[7 + k, s : s + 8, :] for k in range(LEVELS)]

            def cell(f, k):
                return src[j, f * LEVELS + k, s : s + 8, :]

            def around(f, k):
                p = f * LEVELS + k
                c = src[j, p, s : s + 8, :]
                up, lo = src[j, p, s + 1 : s + 9, :], src[j, p, s - 1 : s + 7, :]
                be = pltpu.roll(jnp.where(at_end, src[before, p, s : s + 8, :], c), 1, 1)
                ah = pltpu.roll(jnp.where(at_start, src[after, p, s : s + 8, :], c), LANES - 1, 1)
                return c, up, lo, ah, be

            def rest(parts):
                c, up, lo, ah, be = parts
                return c0 * c + d * (up + lo) + (ga * ah + gb * be)

            def vertical(f, k):
                if k == 0:
                    return cell(f, 1)
                if k == LEVELS - 1:
                    return -cell(f, k - 1)
                return cell(f, k + 1) - cell(f, k - 1)

            for k in range(LEVELS):
                rho, u, v, w, p = (around(f, k) for f in range(5))
                div = (u[1] - u[2]) + (v[3] - v[4]) + vertical(3, k)
                results = (
                    rest(rho) - h * div,
                    rest(u) + s2 * v[0] - h * (p[1] - p[2]),
                    rest(v) - s5 * u[0] - h * (p[3] - p[4]),
                    rest(w) - h * vertical(4, k),
                    rest(p) - stiff[k] * div,
                )
                for f, result in enumerate(results):
                    plane = f * LEVELS + k
                    if base is not None:
                        result = old * base[j, plane, s : s + 8, :] + new * result
                    dst[j, plane, s : s + 8, :] = result
        return carry

    lax.fori_loop(0, nazi, body, 0)


def fill_coefficients(coef, first, shift_ref, spin_ref, drift_ref, stiff_ref):
    count = coef.shape[1] - 2 * HALO
    shape = (count, spin_ref.shape[1])
    radius = lax.broadcasted_iota(jnp.int32, shape, 0) + first
    match = radius == lax.broadcasted_iota(jnp.int32, shape, 1)

    def column(values):
        picked = jnp.sum(jnp.where(match, values, 0.0), axis=1, keepdims=True)
        return jnp.broadcast_to(picked, (count, LANES))

    c = time_step * diffuse
    half = 0.5 * time_step
    inside = column(jnp.ones((1, shape[1]), jnp.float32))
    spin, drift = column(spin_ref[...]), column(drift_ref[...])
    values = [
        (1.0 - 4.0 * c) * inside,
        c * inside,
        c * inside - half * drift,
        c * inside + half * drift,
        half * inside,
        2.0 * time_step * spin,
        half * spin,
    ]
    values += [half * column(stiff_ref[k : k + 1, :]) for k in range(LEVELS)]
    values.append(column(shift_ref[...].astype(jnp.float32)))
    for i, value in enumerate(values):
        coef[i, HALO : HALO + count, :] = value


def compute_kernel(shift_ref, spin_ref, drift_ref, stiff_ref, ext_ref, out_ref, coef_ref, one, two, three):
    nazi, planes, rows, cells = ext_ref.shape
    own_rows = rows - 2 * OWN
    rad, azi = lax.axis_index("rad"), lax.axis_index("azi")
    lane = lax.broadcasted_iota(jnp.int32, (8, LANES), 1)
    wide = range(HALO, rows - HALO, 8)
    own = range(OWN, rows - OWN, 8)
    fill_coefficients(coef_ref, rad * own_rows - HALO, shift_ref, spin_ref, drift_ref, stiff_ref)

    def amounts(s):
        shift = coef_ref[11, s : s + 8, :].astype(jnp.int32)
        return shift // LANES, shift % LANES

    def rotate(here, behind, offsets):
        mixed = jnp.where(lane >= LANES - offsets, behind, here)
        return jnp.take_along_axis(mixed, lax.rem(lane - offsets + LANES, LANES), axis=1)

    stage(ext_ref, None, one, coef_ref, wide, 0.0, 1.0)
    stage(one, ext_ref, two, coef_ref, wide, 0.75, 0.25)
    stage(two, ext_ref, three, coef_ref, wide, 1.0 / 3.0, 2.0 / 3.0)
    for s in wide:
        hops, offsets = amounts(s)

        def shifted(p, carry):
            blocks = [three[b, p, s : s + 8, :] for b in range(nazi)]
            blocks = [rotate(blocks[b], blocks[b - 1], offsets) for b in range(nazi)]
            for bit in range(nazi.bit_length() - 1):
                taken = (hops // (1 << bit)) % 2 == 1
                blocks = [jnp.where(taken, blocks[b - (1 << bit)], blocks[b]) for b in range(nazi)]
            for b in range(nazi):
                one[b, p, s : s + 8, :] = blocks[b]
            return carry

        lax.fori_loop(0, planes, shifted, 0)

    stage(one, None, two, coef_ref, wide, 0.0, 1.0)
    stage(two, one, three, coef_ref, wide, 0.75, 0.25)
    stage(three, one, two, coef_ref, own, 1.0 / 3.0, 2.0 / 3.0)
    for s in own:
        hops, offsets = amounts(s)
        source = lax.rem(azi - hops + nazi, nazi)

        def final(p, carry):
            blocks = [two[b, p, s : s + 8, :] for b in range(nazi)]
            here, behind = blocks[0], blocks[-1]
            for b in range(1, nazi):
                here = jnp.where(source == b, blocks[b], here)
                behind = jnp.where(source == b, blocks[b - 1], behind)
            out_ref[p, s - OWN : s - OWN + 8, :] = rotate(here, behind, offsets)
            return carry

        lax.fori_loop(0, planes, final, 0)


def on_device(state, shifts, spin, drift, stiffness):
    fields, levels, rows, cells = state.shape
    planes = fields * levels
    nrad, nazi = lax.axis_size("rad"), lax.axis_size("azi")
    flat = state.reshape(planes, rows, cells)
    ext = gathered(flat, nrad, nazi)
    whole = pltpu.VMEM(ext.shape, jnp.float32)
    out = pl.pallas_call(
        compute_kernel,
        out_shape=jax.ShapeDtypeStruct(flat.shape, jnp.float32),
        in_specs=[pl.BlockSpec(memory_space=pltpu.VMEM)] * 5,
        out_specs=pl.BlockSpec(memory_space=pltpu.VMEM),
        scratch_shapes=[pltpu.VMEM((12, rows + 2 * OWN, LANES), jnp.float32), whole, whole, whole],
        compiler_params=pltpu.CompilerParams(vmem_limit_bytes=40 * 2**20),
    )(shifts[None], spin[None], drift[None], stiffness, ext)
    return out.reshape(state.shape)


def solution(mesh):
    in_specs = (P(None, None, "rad", "azi"), P(), P(), P(), P())
    out_specs = P(None, None, "rad", "azi")
    return jax.shard_map(
        on_device, mesh=mesh, in_specs=in_specs, out_specs=out_specs, check_vma=False
    )
```

```python
import functools

import jax
import jax.numpy as jnp
from jax import lax
from jax.experimental import pallas as pl
from jax.experimental.pallas import tpu as pltpu
from jax.sharding import PartitionSpec as P

MESH = pl.DeviceIdType.MESH
STEPS = 2
HALO = 8
OWN = 16
LANES = 128
LEVELS = 4
time_step = 0.15
diffuse = 0.05


def gather_kernel(nrad, nazi, x_ref, ext_ref, zeros, own_sem, z_send, z_recv, h_send, h_recv, edge_sem):
    rad, azi = lax.axis_index("rad"), lax.axis_index("azi")
    rows = x_ref.shape[1]
    has_low, has_high = rad > 0, rad < nrad - 1

    has_left, has_right = azi > 0, azi < nazi - 1
    neighbours = ((has_left, rad, azi - 1), (has_right, rad, azi + 1), (has_low, rad - 1, azi), (has_high, rad + 1, azi))

    barrier = pltpu.get_barrier_semaphore()
    expected = 0
    for present, to_rad, to_azi in neighbours:
        expected = expected + present.astype(jnp.int32)

        @pl.when(present)
        def _():
            pl.semaphore_signal(barrier, inc=1, device_id=(to_rad, to_azi), device_id_type=MESH)

    own = pltpu.make_async_copy(x_ref, ext_ref.at[azi, :, pl.ds(OWN, rows)], own_sem)
    own.start()
    zeros[...] = jnp.zeros_like(zeros)
    pl.semaphore_wait(barrier, expected)

    def along(side, t):
        block = azi - t if side == 0 else azi + t
        src = x_ref if t == 0 else ext_ref.at[block, :, pl.ds(OWN, rows)]
        return pltpu.make_async_remote_copy(
            src_ref=src,
            dst_ref=ext_ref.at[block, :, pl.ds(OWN, rows)],
            send_sem=z_send.at[side, t],
            recv_sem=z_recv.at[side, t],
            device_id=(rad, azi + 1 if side == 0 else azi - 1),
            device_id_type=MESH,
        )

    def sends(side, t):
        if side == 0:
            return jnp.logical_and(azi - t >= 0, has_right)
        return jnp.logical_and(azi + t < nazi, has_left)

    def arrives(side, t):
        return azi - 1 - t >= 0 if side == 0 else azi + 1 + t < nazi

    def arrived(side, t):
        block = azi - 1 - t if side == 0 else azi + 1 + t
        return pltpu.make_async_remote_copy(
            src_ref=x_ref,
            dst_ref=ext_ref.at[block, :, pl.ds(OWN, rows)],
            send_sem=z_send.at[side, t],
            recv_sem=z_recv.at[side, t],
            device_id=(rad, azi + 1 if side == 0 else azi - 1),
            device_id_type=MESH,
        )

    def radial(to, block, own_block):
        if to == 0:
            start, there = 0, OWN + rows
        else:
            start, there = rows - HALO, OWN - HALO
        src = x_ref.at[:, pl.ds(start, HALO)] if own_block else ext_ref.at[block, :, pl.ds(OWN + start, HALO)]
        return pltpu.make_async_remote_copy(
            src_ref=src,
            dst_ref=ext_ref.at[block, :, pl.ds(there, HALO)],
            send_sem=h_send.at[to, block],
            recv_sem=h_recv.at[to, block],
            device_id=(rad - 1 if to == 0 else rad + 1, azi),
            device_id_type=MESH,
        )

    def pass_on(block, own_block=False):
        @pl.when(has_low)
        def _():
            radial(0, block, own_block).start()

        @pl.when(has_high)
        def _():
            radial(1, block, own_block).start()

    def edge(b, side):
        start = OWN - HALO if side == 0 else OWN + rows
        return pltpu.make_async_copy(zeros, ext_ref.at[b, :, pl.ds(start, HALO)], edge_sem.at[side, b])

    for side in range(2):

        @pl.when(sends(side, 0))
        def _():
            along(side, 0).start()

    pass_on(azi, True)
    for side, missing in enumerate((has_low, has_high)):

        @pl.when(jnp.logical_not(missing))
        def _():
            for b in range(nazi):
                edge(b, side).start()

    for t in range(nazi - 1):
        for side in range(2):

            @pl.when(arrives(side, t))
            def _():
                arrived(side, t).wait_recv()

                @pl.when(sends(side, t + 1))
                def _():
                    along(side, t + 1).start()

                pass_on(azi - 1 - t if side == 0 else azi + 1 + t)

    for side, missing in enumerate((has_low, has_high)):

        @pl.when(jnp.logical_not(missing))
        def _():
            for b in range(nazi):
                edge(b, side).wait()

    own.wait()
    for t in range(nazi - 1):
        for side in range(2):

            @pl.when(sends(side, t))
            def _():
                along(side, t).wait_send()

    @pl.when(has_low)
    def _():
        for b in range(nazi):
            radial(0, b, False).wait_send()
            radial(1, b, False).wait_recv()

    @pl.when(has_high)
    def _():
        for b in range(nazi):
            radial(1, b, False).wait_send()
            radial(0, b, False).wait_recv()


def gathered(x, nrad, nazi):
    planes, rows, cells = x.shape
    return pl.pallas_call(
        functools.partial(gather_kernel, nrad, nazi),
        out_shape=jax.ShapeDtypeStruct((nazi, planes, rows + 2 * OWN, cells), jnp.float32),
        in_specs=[pl.BlockSpec(memory_space=pl.ANY)],
        out_specs=pl.BlockSpec(memory_space=pltpu.VMEM),
        scratch_shapes=[
            pltpu.VMEM((planes, HALO, cells), jnp.float32),
            pltpu.SemaphoreType.DMA,
            pltpu.SemaphoreType.DMA((2, nazi)),
            pltpu.SemaphoreType.DMA((2, nazi)),
            pltpu.SemaphoreType.DMA((2, nazi)),
            pltpu.SemaphoreType.DMA((2, nazi)),
            pltpu.SemaphoreType.DMA((2, nazi)),
        ],
        compiler_params=pltpu.CompilerParams(
            collective_id=0, has_side_effects=True, vmem_limit_bytes=20 * 2**20
        ),
    )(x)


def tiles_for(first, last):
    starts = list(range(first, last - 6, 8))
    if starts[-1] + 7 < last:
        starts.append(last - 7)
    return starts


def stage(src, base, dst, coef, tiles, old, new):
    nazi = src.shape[0]
    lane = lax.broadcasted_iota(jnp.int32, (8, LANES), 1)
    at_end, at_start = lane == LANES - 1, lane == 0

    def body(j, carry):
        before = lax.rem(j + nazi - 1, nazi)
        after = lax.rem(j + 1, nazi)
        for s in tiles:
            c0, d, ga, gb, h, s2, s5 = (coef[i, s : s + 8, :] for i in range(7))
            stiff = [coef[7 + k, s : s + 8, :] for k in range(LEVELS)]

            def cell(f, k):
                return src[j, f * LEVELS + k, s : s + 8, :]

            def around(f, k):
                p = f * LEVELS + k
                c = src[j, p, s : s + 8, :]
                up, lo = src[j, p, s + 1 : s + 9, :], src[j, p, s - 1 : s + 7, :]
                be = pltpu.roll(jnp.where(at_end, src[before, p, s : s + 8, :], c), 1, 1)
                ah = pltpu.roll(jnp.where(at_start, src[after, p, s : s + 8, :], c), LANES - 1, 1)
                return c, up, lo, ah, be

            def rest(parts):
                c, up, lo, ah, be = parts
                return c0 * c + d * (up + lo) + (ga * ah + gb * be)

            def vertical(f, k):
                if k == 0:
                    return cell(f, 1)
                if k == LEVELS - 1:
                    return -cell(f, k - 1)
                return cell(f, k + 1) - cell(f, k - 1)

            done = {}
            for k in range(LEVELS):
                rho, u, v, w, p = (around(f, k) for f in range(5))
                div = (u[1] - u[2]) + (v[3] - v[4]) + vertical(3, k)
                results = (
                    rest(rho) - h * div,
                    rest(u) + s2 * v[0] - h * (p[1] - p[2]),
                    rest(v) - s5 * u[0] - h * (p[3] - p[4]),
                    rest(w) - h * vertical(4, k),
                    rest(p) - stiff[k] * div,
                )
                for f, result in enumerate(results):
                    plane = f * LEVELS + k
                    if base is not None:
                        result = old * base[j, plane, s : s + 8, :] + new * result
                    done[plane] = result
            for plane, result in done.items():
                dst[j, plane, s : s + 8, :] = result
        return carry

    lax.fori_loop(0, nazi, body, 0)


def fill_coefficients(coef, first, shift_ref, spin_ref, drift_ref, stiff_ref):
    count = coef.shape[1] - 2 * HALO
    shape = (count, spin_ref.shape[1])
    radius = lax.broadcasted_iota(jnp.int32, shape, 0) + first
    match = radius == lax.broadcasted_iota(jnp.int32, shape, 1)

    def column(values):
        picked = jnp.sum(jnp.where(match, values, 0.0), axis=1, keepdims=True)
        return jnp.broadcast_to(picked, (count, LANES))

    c = time_step * diffuse
    half = 0.5 * time_step
    inside = column(jnp.ones((1, shape[1]), jnp.float32))
    spin, drift = column(spin_ref[...]), column(drift_ref[...])
    values = [
        (1.0 - 4.0 * c) * inside,
        c * inside,
        c * inside - half * drift,
        c * inside + half * drift,
        half * inside,
        2.0 * time_step * spin,
        half * spin,
    ]
    values += [half * column(stiff_ref[k : k + 1, :]) for k in range(LEVELS)]
    values.append(column(shift_ref[...].astype(jnp.float32)))
    for i, value in enumerate(values):
        coef[i, HALO : HALO + count, :] = value


def compute_kernel(shift_ref, spin_ref, drift_ref, stiff_ref, ext_ref, out_ref, coef_ref, one, two, three):
    nazi, planes, rows, cells = ext_ref.shape
    own_rows = rows - 2 * OWN
    rad, azi = lax.axis_index("rad"), lax.axis_index("azi")
    lane = lax.broadcasted_iota(jnp.int32, (8, LANES), 1)

    def rows_with(margin):
        return tiles_for(OWN - margin, rows - OWN - 1 + margin)

    fill_coefficients(coef_ref, rad * own_rows - HALO, shift_ref, spin_ref, drift_ref, stiff_ref)

    def amounts(s):
        shift = coef_ref[11, s : s + 8, :].astype(jnp.int32)
        return shift // LANES, shift % LANES

    def rotate(here, behind, offsets):
        mixed = jnp.where(lane >= LANES - offsets, behind, here)
        return jnp.take_along_axis(mixed, lax.rem(lane - offsets + LANES, LANES), axis=1)

    stage(ext_ref, None, one, coef_ref, rows_with(5), 0.0, 1.0)
    stage(one, ext_ref, two, coef_ref, rows_with(4), 0.75, 0.25)
    stage(two, ext_ref, three, coef_ref, rows_with(3), 1.0 / 3.0, 2.0 / 3.0)
    for s in rows_with(3):
        hops, offsets = amounts(s)

        def shifted(p, carry):
            blocks = [three[b, p, s : s + 8, :] for b in range(nazi)]
            blocks = [rotate(blocks[b], blocks[b - 1], offsets) for b in range(nazi)]
            for bit in range(nazi.bit_length() - 1):
                taken = (hops // (1 << bit)) % 2 == 1
                blocks = [jnp.where(taken, blocks[b - (1 << bit)], blocks[b]) for b in range(nazi)]
            for b in range(nazi):
                one[b, p, s : s + 8, :] = blocks[b]
            return carry

        lax.fori_loop(0, planes, shifted, 0)

    stage(one, None, two, coef_ref, rows_with(2), 0.0, 1.0)
    stage(two, one, three, coef_ref, rows_with(1), 0.75, 0.25)
    stage(three, one, two, coef_ref, rows_with(0), 1.0 / 3.0, 2.0 / 3.0)
    for s in rows_with(0):
        hops, offsets = amounts(s)
        source = lax.rem(azi - hops + nazi, nazi)

        def final(p, carry):
            blocks = [two[b, p, s : s + 8, :] for b in range(nazi)]
            here, behind = blocks[0], blocks[-1]
            for b in range(1, nazi):
                here = jnp.where(source == b, blocks[b], here)
                behind = jnp.where(source == b, blocks[b - 1], behind)
            out_ref[p, s - OWN : s - OWN + 8, :] = rotate(here, behind, offsets)
            return carry

        lax.fori_loop(0, planes, final, 0)


def on_device(state, shifts, spin, drift, stiffness):
    fields, levels, rows, cells = state.shape
    planes = fields * levels
    nrad, nazi = lax.axis_size("rad"), lax.axis_size("azi")
    flat = state.reshape(planes, rows, cells)
    ext = gathered(flat, nrad, nazi)
    whole = pltpu.VMEM(ext.shape, jnp.float32)
    out = pl.pallas_call(
        compute_kernel,
        out_shape=jax.ShapeDtypeStruct(flat.shape, jnp.float32),
        in_specs=[pl.BlockSpec(memory_space=pltpu.VMEM)] * 5,
        out_specs=pl.BlockSpec(memory_space=pltpu.VMEM),
        scratch_shapes=[pltpu.VMEM((12, rows + 2 * OWN, LANES), jnp.float32), whole, whole, whole],
        compiler_params=pltpu.CompilerParams(vmem_limit_bytes=40 * 2**20),
    )(shifts[None], spin[None], drift[None], stiffness, ext)
    return out.reshape(state.shape)


def solution(mesh):
    in_specs = (P(None, None, "rad", "azi"), P(), P(), P(), P())
    out_specs = P(None, None, "rad", "azi")
    return jax.shard_map(
        on_device, mesh=mesh, in_specs=in_specs, out_specs=out_specs, check_vma=False
    )
```

```python
import functools

import jax
import jax.numpy as jnp
from jax import lax
from jax.experimental import pallas as pl
from jax.experimental.pallas import tpu as pltpu
from jax.sharding import PartitionSpec as P

MESH = pl.DeviceIdType.MESH
STEPS = 2
HALO = 8
OWN = 16
LANES = 128
LEVELS = 4
time_step = 0.15
diffuse = 0.05


def gather_kernel(nrad, nazi, x_ref, ext_ref, zeros, own_sem, z_send, z_recv, h_send, h_recv, edge_sem):
    rad, azi = lax.axis_index("rad"), lax.axis_index("azi")
    rows = x_ref.shape[1]
    has_low, has_high = rad > 0, rad < nrad - 1

    has_left, has_right = azi > 0, azi < nazi - 1
    neighbours = ((has_left, rad, azi - 1), (has_right, rad, azi + 1), (has_low, rad - 1, azi), (has_high, rad + 1, azi))

    barrier = pltpu.get_barrier_semaphore()
    expected = 0
    for present, to_rad, to_azi in neighbours:
        expected = expected + present.astype(jnp.int32)

        @pl.when(present)
        def _():
            pl.semaphore_signal(barrier, inc=1, device_id=(to_rad, to_azi), device_id_type=MESH)

    own = pltpu.make_async_copy(x_ref, ext_ref.at[azi, :, pl.ds(OWN, rows)], own_sem)
    own.start()
    zeros[...] = jnp.zeros_like(zeros)
    pl.semaphore_wait(barrier, expected)

    def along(side, t):
        block = azi - t if side == 0 else azi + t
        src = x_ref if t == 0 else ext_ref.at[block, :, pl.ds(OWN, rows)]
        return pltpu.make_async_remote_copy(
            src_ref=src,
            dst_ref=ext_ref.at[block, :, pl.ds(OWN, rows)],
            send_sem=z_send.at[side, t],
            recv_sem=z_recv.at[side, t],
            device_id=(rad, azi + 1 if side == 0 else azi - 1),
            device_id_type=MESH,
        )

    def sends(side, t):
        if side == 0:
            return jnp.logical_and(azi - t >= 0, has_right)
        return jnp.logical_and(azi + t < nazi, has_left)

    def arrives(side, t):
        return azi - 1 - t >= 0 if side == 0 else azi + 1 + t < nazi

    def arrived(side, t):
        block = azi - 1 - t if side == 0 else azi + 1 + t
        return pltpu.make_async_remote_copy(
            src_ref=x_ref,
            dst_ref=ext_ref.at[block, :, pl.ds(OWN, rows)],
            send_sem=z_send.at[side, t],
            recv_sem=z_recv.at[side, t],
            device_id=(rad, azi + 1 if side == 0 else azi - 1),
            device_id_type=MESH,
        )

    def radial(to, block, own_block):
        if to == 0:
            start, there = 0, OWN + rows
        else:
            start, there = rows - HALO, OWN - HALO
        src = x_ref.at[:, pl.ds(start, HALO)] if own_block else ext_ref.at[block, :, pl.ds(OWN + start, HALO)]
        return pltpu.make_async_remote_copy(
            src_ref=src,
            dst_ref=ext_ref.at[block, :, pl.ds(there, HALO)],
            send_sem=h_send.at[to, block],
            recv_sem=h_recv.at[to, block],
            device_id=(rad - 1 if to == 0 else rad + 1, azi),
            device_id_type=MESH,
        )

    def pass_on(block, own_block=False):
        @pl.when(has_low)
        def _():
            radial(0, block, own_block).start()

        @pl.when(has_high)
        def _():
            radial(1, block, own_block).start()

    def edge(b, side):
        start = OWN - HALO if side == 0 else OWN + rows
        return pltpu.make_async_copy(zeros, ext_ref.at[b, :, pl.ds(start, HALO)], edge_sem.at[side, b])

    for side in range(2):

        @pl.when(sends(side, 0))
        def _():
            along(side, 0).start()

    pass_on(azi, True)
    for side, missing in enumerate((has_low, has_high)):

        @pl.when(jnp.logical_not(missing))
        def _():
            for b in range(nazi):
                edge(b, side).start()

    for t in range(nazi - 1):
        for side in range(2):

            @pl.when(arrives(side, t))
            def _():
                arrived(side, t).wait_recv()

                @pl.when(sends(side, t + 1))
                def _():
                    along(side, t + 1).start()

                pass_on(azi - 1 - t if side == 0 else azi + 1 + t)

    for side, missing in enumerate((has_low, has_high)):

        @pl.when(jnp.logical_not(missing))
        def _():
            for b in range(nazi):
                edge(b, side).wait()

    own.wait()
    for t in range(nazi - 1):
        for side in range(2):

            @pl.when(sends(side, t))
            def _():
                along(side, t).wait_send()

    @pl.when(has_low)
    def _():
        for b in range(nazi):
            radial(0, b, False).wait_send()
            radial(1, b, False).wait_recv()

    @pl.when(has_high)
    def _():
        for b in range(nazi):
            radial(1, b, False).wait_send()
            radial(0, b, False).wait_recv()


def gathered(x, nrad, nazi):
    planes, rows, cells = x.shape
    return pl.pallas_call(
        functools.partial(gather_kernel, nrad, nazi),
        out_shape=jax.ShapeDtypeStruct((nazi, planes, rows + 2 * OWN, cells), jnp.float32),
        in_specs=[pl.BlockSpec(memory_space=pltpu.HBM)],
        out_specs=pl.BlockSpec(memory_space=pltpu.VMEM),
        scratch_shapes=[
            pltpu.VMEM((planes, HALO, cells), jnp.float32),
            pltpu.SemaphoreType.DMA,
            pltpu.SemaphoreType.DMA((2, nazi)),
            pltpu.SemaphoreType.DMA((2, nazi)),
            pltpu.SemaphoreType.DMA((2, nazi)),
            pltpu.SemaphoreType.DMA((2, nazi)),
            pltpu.SemaphoreType.DMA((2, nazi)),
        ],
        compiler_params=pltpu.CompilerParams(
            collective_id=0, has_side_effects=True, vmem_limit_bytes=20 * 2**20
        ),
    )(x)


def tiles_for(first, last):
    starts = list(range(first, last - 6, 8))
    if starts[-1] + 7 < last:
        starts.append(last - 7)
    return starts


def stage(src, base, dst, coef, tiles, old, new):
    nazi = src.shape[0]
    lane = lax.broadcasted_iota(jnp.int32, (8, LANES), 1)
    at_end, at_start = lane == LANES - 1, lane == 0

    def body(j, carry):
        before = lax.rem(j + nazi - 1, nazi)
        after = lax.rem(j + 1, nazi)
        for s in tiles:
            c0, d, ga, gb, h, s2, s5 = (coef[i, s : s + 8, :] for i in range(7))
            stiff = [coef[7 + k, s : s + 8, :] for k in range(LEVELS)]

            def cell(f, k):
                return src[j, f * LEVELS + k, s : s + 8, :]

            def around(f, k):
                p = f * LEVELS + k
                c = src[j, p, s : s + 8, :]
                up, lo = src[j, p, s + 1 : s + 9, :], src[j, p, s - 1 : s + 7, :]
                be = pltpu.roll(jnp.where(at_end, src[before, p, s : s + 8, :], c), 1, 1)
                ah = pltpu.roll(jnp.where(at_start, src[after, p, s : s + 8, :], c), LANES - 1, 1)
                return c, up, lo, ah, be

            def rest(parts):
                c, up, lo, ah, be = parts
                return c0 * c + d * (up + lo) + (ga * ah + gb * be)

            def vertical(f, k):
                if k == 0:
                    return cell(f, 1)
                if k == LEVELS - 1:
                    return -cell(f, k - 1)
                return cell(f, k + 1) - cell(f, k - 1)

            done = {}
            for k in range(LEVELS):
                rho, u, v, w, p = (around(f, k) for f in range(5))
                div = (u[1] - u[2]) + (v[3] - v[4]) + vertical(3, k)
                results = (
                    rest(rho) - h * div,
                    rest(u) + s2 * v[0] - h * (p[1] - p[2]),
                    rest(v) - s5 * u[0] - h * (p[3] - p[4]),
                    rest(w) - h * vertical(4, k),
                    rest(p) - stiff[k] * div,
                )
                for f, result in enumerate(results):
                    plane = f * LEVELS + k
                    if base is not None:
                        result = old * base[j, plane, s : s + 8, :] + new * result
                    done[plane] = result
            for plane, result in done.items():
                dst[j, plane, s : s + 8, :] = result
        return carry

    lax.fori_loop(0, nazi, body, 0)


def fill_coefficients(coef, first, shift_ref, spin_ref, drift_ref, stiff_ref):
    count = coef.shape[1] - 2 * HALO
    shape = (count, spin_ref.shape[1])
    radius = lax.broadcasted_iota(jnp.int32, shape, 0) + first
    match = radius == lax.broadcasted_iota(jnp.int32, shape, 1)

    def column(values):
        picked = jnp.sum(jnp.where(match, values, 0.0), axis=1, keepdims=True)
        return jnp.broadcast_to(picked, (count, LANES))

    c = time_step * diffuse
    half = 0.5 * time_step
    inside = column(jnp.ones((1, shape[1]), jnp.float32))
    spin, drift = column(spin_ref[...]), column(drift_ref[...])
    values = [
        (1.0 - 4.0 * c) * inside,
        c * inside,
        c * inside - half * drift,
        c * inside + half * drift,
        half * inside,
        2.0 * time_step * spin,
        half * spin,
    ]
    values += [half * column(stiff_ref[k : k + 1, :]) for k in range(LEVELS)]
    values.append(column(shift_ref[...].astype(jnp.float32)))
    for i, value in enumerate(values):
        coef[i, HALO : HALO + count, :] = value


def compute_kernel(shift_ref, spin_ref, drift_ref, stiff_ref, ext_ref, out_ref, coef_ref, one, two, three):
    nazi, planes, rows, cells = ext_ref.shape
    own_rows = rows - 2 * OWN
    rad, azi = lax.axis_index("rad"), lax.axis_index("azi")
    lane = lax.broadcasted_iota(jnp.int32, (8, LANES), 1)

    def rows_with(margin):
        return tiles_for(OWN - margin, rows - OWN - 1 + margin)

    group = max(1, planes * 4 // max(nazi, 4))
    fill_coefficients(coef_ref, rad * own_rows - HALO, shift_ref, spin_ref, drift_ref, stiff_ref)

    def amounts(s):
        shift = coef_ref[11, s : s + 8, :].astype(jnp.int32)
        return shift // LANES, shift % LANES

    def rotate(here, behind, offsets):
        mixed = jnp.where(lane >= LANES - offsets, behind, here)
        return jnp.take_along_axis(mixed, lax.rem(lane - offsets + LANES, LANES), axis=1)

    stage(ext_ref, None, one, coef_ref, rows_with(5), 0.0, 1.0)
    stage(one, ext_ref, two, coef_ref, rows_with(4), 0.75, 0.25)
    stage(two, ext_ref, three, coef_ref, rows_with(3), 1.0 / 3.0, 2.0 / 3.0)
    for s in rows_with(3):
        hops, offsets = amounts(s)

        def shifted(p, carry):
            blocks = [three[b, p, s : s + 8, :] for b in range(nazi)]
            blocks = [rotate(blocks[b], blocks[b - 1], offsets) for b in range(nazi)]
            for bit in range(nazi.bit_length() - 1):
                taken = (hops // (1 << bit)) % 2 == 1
                blocks = [jnp.where(taken, blocks[b - (1 << bit)], blocks[b]) for b in range(nazi)]
            for b in range(nazi):
                one[b, p, s : s + 8, :] = blocks[b]
            return carry

        lax.fori_loop(0, planes, shifted, 0, unroll=group)

    stage(one, None, two, coef_ref, rows_with(2), 0.0, 1.0)
    stage(two, one, three, coef_ref, rows_with(1), 0.75, 0.25)
    stage(three, one, two, coef_ref, rows_with(0), 1.0 / 3.0, 2.0 / 3.0)
    for s in rows_with(0):
        hops, offsets = amounts(s)
        source = lax.rem(azi - hops + nazi, nazi)

        def final(p, carry):
            blocks = [two[b, p, s : s + 8, :] for b in range(nazi)]
            here, behind = blocks[0], blocks[-1]
            for b in range(1, nazi):
                here = jnp.where(source == b, blocks[b], here)
                behind = jnp.where(source == b, blocks[b - 1], behind)
            out_ref[p, s - OWN : s - OWN + 8, :] = rotate(here, behind, offsets)
            return carry

        lax.fori_loop(0, planes, final, 0, unroll=group)


def on_device(state, shifts, spin, drift, stiffness):
    fields, levels, rows, cells = state.shape
    planes = fields * levels
    nrad, nazi = lax.axis_size("rad"), lax.axis_size("azi")
    flat = state.reshape(planes, rows, cells)
    ext = gathered(flat, nrad, nazi)
    whole = pltpu.VMEM(ext.shape, jnp.float32)
    out = pl.pallas_call(
        compute_kernel,
        out_shape=jax.ShapeDtypeStruct(flat.shape, jnp.float32),
        in_specs=[pl.BlockSpec(memory_space=pltpu.VMEM)] * 5,
        out_specs=pl.BlockSpec(memory_space=pltpu.VMEM),
        scratch_shapes=[pltpu.VMEM((12, rows + 2 * OWN, LANES), jnp.float32), whole, whole, whole],
        compiler_params=pltpu.CompilerParams(vmem_limit_bytes=40 * 2**20),
    )(shifts[None], spin[None], drift[None], stiffness, ext)
    return out.reshape(state.shape)


def solution(mesh):
    in_specs = (P(None, None, "rad", "azi"), P(), P(), P(), P())
    out_specs = P(None, None, "rad", "azi")
    return jax.shard_map(
        on_device, mesh=mesh, in_specs=in_specs, out_specs=out_specs, check_vma=False
    )
```

```python
import functools

import jax
import jax.numpy as jnp
from jax import lax
from jax.experimental import pallas as pl
from jax.experimental.pallas import tpu as pltpu
from jax.sharding import PartitionSpec as P

MESH = pl.DeviceIdType.MESH
STEPS = 2
HALO = 8
OWN = 16
LANES = 128
LEVELS = 4
time_step = 0.15
diffuse = 0.05


def tiles_for(first, last):
    starts = list(range(first, last - 6, 8))
    if starts[-1] + 7 < last:
        starts.append(last - 7)
    return starts


def stage(src, base, dst, coef, tiles, old, new):
    nazi = src.shape[0]
    lane = lax.broadcasted_iota(jnp.int32, (LEVELS, 8, LANES), 2)
    at_end, at_start = lane == LANES - 1, lane == 0

    def body(j, carry):
        before = lax.rem(j + nazi - 1, nazi)
        after = lax.rem(j + 1, nazi)
        for s in tiles:
            c0, d, ga, gb, h, s2, s5 = (coef[i, s : s + 8, :] for i in range(7))
            stiff = coef[7 : 7 + LEVELS, s : s + 8, :]

            def around(f):
                p = slice(f * LEVELS, (f + 1) * LEVELS)
                c = src[j, p, s : s + 8, :]
                up, lo = src[j, p, s + 1 : s + 9, :], src[j, p, s - 1 : s + 7, :]
                be = pltpu.roll(jnp.where(at_end, src[before, p, s : s + 8, :], c), 1, 2)
                ah = pltpu.roll(jnp.where(at_start, src[after, p, s : s + 8, :], c), LANES - 1, 2)
                return c, up, lo, ah, be

            def rest(parts):
                c, up, lo, ah, be = parts
                return c0 * c + d * (up + lo) + (ga * ah + gb * be)

            def vertical(c):
                middle = c[2:] - c[:-2]
                return jnp.concatenate([c[1:2], middle, -c[LEVELS - 2 : LEVELS - 1]], axis=0)

            rho, u, v, w, p = (around(f) for f in range(5))
            div = (u[1] - u[2]) + (v[3] - v[4]) + vertical(w[0])
            results = (
                rest(rho) - h * div,
                rest(u) + s2 * v[0] - h * (p[1] - p[2]),
                rest(v) - s5 * u[0] - h * (p[3] - p[4]),
                rest(w) - h * vertical(p[0]),
                rest(p) - stiff * div,
            )
            for f, result in enumerate(results):
                planes = slice(f * LEVELS, (f + 1) * LEVELS)
                if base is not None:
                    result = old * base[j, planes, s : s + 8, :] + new * result
                dst[j, planes, s : s + 8, :] = result
        return carry

    lax.fori_loop(0, nazi, body, 0)


def fill_coefficients(coef, first, shift_ref, spin_ref, drift_ref, stiff_ref):
    count = coef.shape[1] - 2 * HALO
    shape = (count, spin_ref.shape[1])
    radius = lax.broadcasted_iota(jnp.int32, shape, 0) + first
    match = radius == lax.broadcasted_iota(jnp.int32, shape, 1)

    def column(values):
        picked = jnp.sum(jnp.where(match, values, 0.0), axis=1, keepdims=True)
        return jnp.broadcast_to(picked, (count, LANES))

    c = time_step * diffuse
    half = 0.5 * time_step
    inside = column(jnp.ones((1, shape[1]), jnp.float32))
    spin, drift = column(spin_ref[...]), column(drift_ref[...])
    values = [
        (1.0 - 4.0 * c) * inside,
        c * inside,
        c * inside - half * drift,
        c * inside + half * drift,
        half * inside,
        2.0 * time_step * spin,
        half * spin,
    ]
    values += [half * column(stiff_ref[k : k + 1, :]) for k in range(LEVELS)]
    values.append(column(shift_ref[...].astype(jnp.float32)))
    for i, value in enumerate(values):
        coef[i, HALO : HALO + count, :] = value


def first_kernel(
    nrad, nazi, shift_ref, spin_ref, drift_ref, stiff_ref, x_ref, sect_ref, coef_ref,
    ext_ref, one, two, own_sem, z_send, z_recv, h_send, h_recv,
):
    rad, azi = lax.axis_index("rad"), lax.axis_index("azi")
    rows = x_ref.shape[1]
    odd = lax.rem(rad, 2)
    has_left, has_right = azi > 0, azi < nazi - 1

    def upper(c):
        return 1 - lax.rem(odd + c, 2)

    def peer(c):
        return rad + (1 - 2 * odd) * (1 - 2 * c)

    has_other = jnp.logical_and(peer(1) >= 0, peer(1) < nrad)

    def half_at(c, offset):
        return pl.ds(pl.multiple_of(HALO * upper(c) + offset, HALO), HALO)

    barrier = pltpu.get_barrier_semaphore()
    expected = 1
    pl.semaphore_signal(barrier, inc=1, device_id=(peer(0), azi), device_id_type=MESH)
    for present, to_rad, to_azi in ((has_left, rad, azi - 1), (has_right, rad, azi + 1), (has_other, peer(1), azi)):
        expected = expected + present.astype(jnp.int32)

        @pl.when(present)
        def _():
            pl.semaphore_signal(barrier, inc=1, device_id=(to_rad, to_azi), device_id_type=MESH)

    own = pltpu.make_async_copy(x_ref, ext_ref.at[azi, :, pl.ds(OWN, rows)], own_sem)
    own.start()
    fill_coefficients(coef_ref, rad * rows - HALO, shift_ref, spin_ref, drift_ref, stiff_ref)

    @pl.when(jnp.logical_not(has_other))
    def _():
        start = pl.multiple_of(OWN - HALO + (HALO + rows) * upper(1), HALO)
        for b in range(nazi):
            ext_ref[b, :, pl.ds(start, HALO), :] = jnp.zeros((x_ref.shape[0], HALO, LANES), jnp.float32)

    pl.semaphore_wait(barrier, expected)

    def z_copy(side, t, c, block, src):
        return pltpu.make_async_remote_copy(
            src_ref=src,
            dst_ref=ext_ref.at[block, :, half_at(c, OWN)],
            send_sem=z_send.at[side, t, c],
            recv_sem=z_recv.at[side, t, c],
            device_id=(rad, azi + 1 if side == 0 else azi - 1),
            device_id_type=MESH,
        )

    def along(side, t, c):
        block = azi - t if side == 0 else azi + t
        src = x_ref.at[:, half_at(c, 0)] if t == 0 else ext_ref.at[block, :, half_at(c, OWN)]
        return z_copy(side, t, c, block, src)

    def came(side, t):
        return azi - 1 - t if side == 0 else azi + 1 + t

    def arrived(side, t, c):
        return z_copy(side, t, c, came(side, t), x_ref.at[:, half_at(c, 0)])

    def last(side):
        return azi if side == 0 else nazi - 1 - azi

    def sends(side, t):
        return jnp.logical_and(t <= last(side), has_right if side == 0 else has_left)

    def arrives(side, t):
        return came(side, t) >= 0 if side == 0 else came(side, t) < nazi

    def radial(c, block, src):
        there = pl.multiple_of(OWN + rows - (HALO + rows) * upper(c), HALO)
        return pltpu.make_async_remote_copy(
            src_ref=src,
            dst_ref=ext_ref.at[block, :, pl.ds(there, HALO)],
            send_sem=h_send.at[c, block],
            recv_sem=h_recv.at[c, block],
            device_id=(peer(c), azi),
            device_id_type=MESH,
        )

    def radial_in(c, block):
        here = pl.multiple_of(OWN - HALO + (HALO + rows) * upper(c), HALO)
        return pltpu.make_async_remote_copy(
            src_ref=x_ref.at[:, half_at(c, 0)],
            dst_ref=ext_ref.at[block, :, pl.ds(here, HALO)],
            send_sem=h_send.at[c, block],
            recv_sem=h_recv.at[c, block],
            device_id=(peer(c), azi),
            device_id_type=MESH,
        )

    def pass_on(c, block, own_block=False):
        src = x_ref.at[:, half_at(c, 0)] if own_block else ext_ref.at[block, :, half_at(c, OWN)]
        if c == 0:
            radial(c, block, src).start()
        else:

            @pl.when(has_other)
            def _():
                radial(c, block, src).start()

    def send(side, t):
        @pl.when(sends(side, t))
        def _():
            along(side, t, 0).start()

            @pl.when(last(side) == t)
            def _():
                along(side, 0, 1).start()

    def step(t, c):
        for side in range(2):

            @pl.when(arrives(side, t))
            def _():
                arrived(side, t, c).wait_recv()
                if c == 0:
                    send(side, t + 1)
                else:

                    @pl.when(sends(side, t + 1))
                    def _():
                        along(side, t + 1, c).start()

                pass_on(c, came(side, t))

    def both(even_rows, odd_rows, src, base, dst, old, new):
        for parity, (start, end) in enumerate((even_rows, odd_rows)):

            @pl.when(odd == parity)
            def _():
                stage(src, base, dst, coef_ref, tiles_for(start, end), old, new)

    low, high, middle = OWN, OWN + rows - 1, OWN + HALO
    third = (1.0 / 3.0, 2.0 / 3.0)

    for side in range(2):
        send(side, 0)
    pass_on(0, azi, True)
    pass_on(1, azi, True)
    for t in range(nazi - 1):
        step(t, 0)
    own.wait()
    for b in range(nazi):
        radial_in(0, b).wait_recv()
    for t in range(max(3, nazi - 1)):
        if t == 0:
            both((middle + 1, high + 5), (low - 5, middle - 2), ext_ref, None, one, 0.0, 1.0)
        if t == 1:
            both((middle + 2, high + 4), (low - 4, middle - 3), one, ext_ref, two, 0.75, 0.25)
        if t == 2:
            both((middle + 3, high + 3), (low - 3, middle - 4), two, ext_ref, sect_ref, *third)
        if t < nazi - 1:
            step(t, 1)

    @pl.when(has_other)
    def _():
        for b in range(nazi):
            radial_in(1, b).wait_recv()

    both((low - 5, middle), (middle - 1, high + 5), ext_ref, None, one, 0.0, 1.0)
    both((low - 4, middle + 1), (middle - 2, high + 4), one, ext_ref, two, 0.75, 0.25)
    both((low - 3, middle + 2), (middle - 3, high + 3), two, ext_ref, sect_ref, *third)

    for c in range(2):
        for t in range(nazi - 1):
            for side in range(2):

                @pl.when(sends(side, t))
                def _():
                    along(side, t, c).wait_send()

    for b in range(nazi):
        radial_in(0, b).wait_send()

    @pl.when(has_other)
    def _():
        for b in range(nazi):
            radial_in(1, b).wait_send()


def second_kernel(sect_ref, coef_ref, out_ref, one, two, three):
    nazi, planes, rows, cells = sect_ref.shape
    azi = lax.axis_index("azi")
    lane = lax.broadcasted_iota(jnp.int32, (8, LANES), 1)

    def rows_with(margin):
        return tiles_for(OWN - margin, rows - OWN - 1 + margin)

    group = max(1, planes * 4 // max(nazi, 4))

    def amounts(s):
        shift = coef_ref[11, s : s + 8, :].astype(jnp.int32)
        return shift // LANES, shift % LANES

    def rotate(here, behind, offsets):
        mixed = jnp.where(lane >= LANES - offsets, behind, here)
        return jnp.take_along_axis(mixed, lax.rem(lane - offsets + LANES, LANES), axis=1)

    for s in rows_with(3):
        hops, offsets = amounts(s)

        def shifted(p, carry):
            blocks = [sect_ref[b, p, s : s + 8, :] for b in range(nazi)]
            blocks = [rotate(blocks[b], blocks[b - 1], offsets) for b in range(nazi)]
            for bit in range(nazi.bit_length() - 1):
                taken = (hops // (1 << bit)) % 2 == 1
                blocks = [jnp.where(taken, blocks[b - (1 << bit)], blocks[b]) for b in range(nazi)]
            for b in range(nazi):
                one[b, p, s : s + 8, :] = blocks[b]
            return carry

        lax.fori_loop(0, planes, shifted, 0, unroll=group)

    stage(one, None, two, coef_ref, rows_with(2), 0.0, 1.0)
    stage(two, one, three, coef_ref, rows_with(1), 0.75, 0.25)
    stage(three, one, two, coef_ref, rows_with(0), 1.0 / 3.0, 2.0 / 3.0)
    for s in rows_with(0):
        hops, offsets = amounts(s)
        source = lax.rem(azi - hops + nazi, nazi)

        def final(p, carry):
            blocks = [two[b, p, s : s + 8, :] for b in range(nazi)]
            here, behind = blocks[0], blocks[-1]
            for b in range(1, nazi):
                here = jnp.where(source == b, blocks[b], here)
                behind = jnp.where(source == b, blocks[b - 1], behind)
            out_ref[p, s - OWN : s - OWN + 8, :] = rotate(here, behind, offsets)
            return carry

        lax.fori_loop(0, planes, final, 0, unroll=group)


def on_device(state, shifts, spin, drift, stiffness):
    fields, levels, rows, cells = state.shape
    planes = fields * levels
    nrad, nazi = lax.axis_size("rad"), lax.axis_size("azi")
    flat = state.reshape(planes, rows, cells)
    whole_shape = (nazi, planes, rows + 2 * OWN, cells)
    coef_shape = (12, rows + 2 * OWN, cells)
    whole = pltpu.VMEM(whole_shape, jnp.float32)
    vmem = pl.BlockSpec(memory_space=pltpu.VMEM)
    dma = pltpu.SemaphoreType.DMA
    sect, coef = pl.pallas_call(
        functools.partial(first_kernel, nrad, nazi),
        out_shape=(
            jax.ShapeDtypeStruct(whole_shape, jnp.float32),
            jax.ShapeDtypeStruct(coef_shape, jnp.float32),
        ),
        in_specs=[vmem] * 4 + [pl.BlockSpec(memory_space=pl.ANY)],
        out_specs=(vmem, vmem),
        scratch_shapes=[
            whole,
            whole,
            whole,
            dma,
            dma((2, nazi, 2)),
            dma((2, nazi, 2)),
            dma((2, nazi)),
            dma((2, nazi)),
        ],
        compiler_params=pltpu.CompilerParams(
            collective_id=0, has_side_effects=True, vmem_limit_bytes=40 * 2**20
        ),
    )(shifts[None], spin[None], drift[None], stiffness, flat)
    out = pl.pallas_call(
        second_kernel,
        out_shape=jax.ShapeDtypeStruct(flat.shape, jnp.float32),
        in_specs=[vmem, vmem],
        out_specs=vmem,
        scratch_shapes=[whole, whole, whole],
        compiler_params=pltpu.CompilerParams(vmem_limit_bytes=40 * 2**20),
    )(sect, coef)
    return out.reshape(state.shape)


def solution(mesh):
    in_specs = (P(None, None, "rad", "azi"), P(), P(), P(), P())
    out_specs = P(None, None, "rad", "azi")
    return jax.shard_map(
        on_device, mesh=mesh, in_specs=in_specs, out_specs=out_specs, check_vma=False
    )
```

```python
import functools

import jax
import jax.numpy as jnp
from jax import lax
from jax.experimental import pallas as pl
from jax.experimental.pallas import tpu as pltpu
from jax.sharding import PartitionSpec as P

MESH = pl.DeviceIdType.MESH
STEPS = 2
HALO = 8
OWN = 16
LANES = 128
LEVELS = 4
time_step = 0.15
diffuse = 0.05


def gather_kernel(nrad, nazi, x_ref, ext_ref, zeros, own_sem, z_send, z_recv, h_send, h_recv, edge_sem):
    rad, azi = lax.axis_index("rad"), lax.axis_index("azi")
    rows = x_ref.shape[1]
    has_low, has_high = rad > 0, rad < nrad - 1

    has_left, has_right = azi > 0, azi < nazi - 1
    neighbours = ((has_left, rad, azi - 1), (has_right, rad, azi + 1), (has_low, rad - 1, azi), (has_high, rad + 1, azi))

    barrier = pltpu.get_barrier_semaphore()
    expected = 0
    for present, to_rad, to_azi in neighbours:
        expected = expected + present.astype(jnp.int32)

        @pl.when(present)
        def _():
            pl.semaphore_signal(barrier, inc=1, device_id=(to_rad, to_azi), device_id_type=MESH)

    own = pltpu.make_async_copy(x_ref, ext_ref.at[azi, :, pl.ds(OWN, rows)], own_sem)
    own.start()
    zeros[...] = jnp.zeros_like(zeros)
    pl.semaphore_wait(barrier, expected)

    def along(side, t):
        block = azi - t if side == 0 else azi + t
        src = x_ref if t == 0 else ext_ref.at[block, :, pl.ds(OWN, rows)]
        return pltpu.make_async_remote_copy(
            src_ref=src,
            dst_ref=ext_ref.at[block, :, pl.ds(OWN, rows)],
            send_sem=z_send.at[side, t],
            recv_sem=z_recv.at[side, t],
            device_id=(rad, azi + 1 if side == 0 else azi - 1),
            device_id_type=MESH,
        )

    def sends(side, t):
        if side == 0:
            return jnp.logical_and(azi - t >= 0, has_right)
        return jnp.logical_and(azi + t < nazi, has_left)

    def arrives(side, t):
        return azi - 1 - t >= 0 if side == 0 else azi + 1 + t < nazi

    def arrived(side, t):
        block = azi - 1 - t if side == 0 else azi + 1 + t
        return pltpu.make_async_remote_copy(
            src_ref=x_ref,
            dst_ref=ext_ref.at[block, :, pl.ds(OWN, rows)],
            send_sem=z_send.at[side, t],
            recv_sem=z_recv.at[side, t],
            device_id=(rad, azi + 1 if side == 0 else azi - 1),
            device_id_type=MESH,
        )

    def radial(to, block, own_block):
        if to == 0:
            start, there = 0, OWN + rows
        else:
            start, there = rows - HALO, OWN - HALO
        src = x_ref.at[:, pl.ds(start, HALO)] if own_block else ext_ref.at[block, :, pl.ds(OWN + start, HALO)]
        return pltpu.make_async_remote_copy(
            src_ref=src,
            dst_ref=ext_ref.at[block, :, pl.ds(there, HALO)],
            send_sem=h_send.at[to, block],
            recv_sem=h_recv.at[to, block],
            device_id=(rad - 1 if to == 0 else rad + 1, azi),
            device_id_type=MESH,
        )

    def pass_on(block, own_block=False):
        @pl.when(has_low)
        def _():
            radial(0, block, own_block).start()

        @pl.when(has_high)
        def _():
            radial(1, block, own_block).start()

    def edge(b, side):
        start = OWN - HALO if side == 0 else OWN + rows
        return pltpu.make_async_copy(zeros, ext_ref.at[b, :, pl.ds(start, HALO)], edge_sem.at[side, b])

    for side in range(2):

        @pl.when(sends(side, 0))
        def _():
            along(side, 0).start()

    pass_on(azi, True)
    for side, missing in enumerate((has_low, has_high)):

        @pl.when(jnp.logical_not(missing))
        def _():
            for b in range(nazi):
                edge(b, side).start()

    for t in range(nazi - 1):
        for side in range(2):

            @pl.when(arrives(side, t))
            def _():
                arrived(side, t).wait_recv()

                @pl.when(sends(side, t + 1))
                def _():
                    along(side, t + 1).start()

                pass_on(azi - 1 - t if side == 0 else azi + 1 + t)

    for side, missing in enumerate((has_low, has_high)):

        @pl.when(jnp.logical_not(missing))
        def _():
            for b in range(nazi):
                edge(b, side).wait()

    own.wait()
    for t in range(nazi - 1):
        for side in range(2):

            @pl.when(sends(side, t))
            def _():
                along(side, t).wait_send()

    @pl.when(has_low)
    def _():
        for b in range(nazi):
            radial(0, b, False).wait_send()
            radial(1, b, False).wait_recv()

    @pl.when(has_high)
    def _():
        for b in range(nazi):
            radial(1, b, False).wait_send()
            radial(0, b, False).wait_recv()


def gathered(x, nrad, nazi):
    planes, rows, cells = x.shape
    return pl.pallas_call(
        functools.partial(gather_kernel, nrad, nazi),
        out_shape=jax.ShapeDtypeStruct((nazi, planes, rows + 2 * OWN, cells), jnp.float32),
        in_specs=[pl.BlockSpec(memory_space=pltpu.HBM)],
        out_specs=pl.BlockSpec(memory_space=pltpu.VMEM),
        scratch_shapes=[
            pltpu.VMEM((planes, HALO, cells), jnp.float32),
            pltpu.SemaphoreType.DMA,
            pltpu.SemaphoreType.DMA((2, nazi)),
            pltpu.SemaphoreType.DMA((2, nazi)),
            pltpu.SemaphoreType.DMA((2, nazi)),
            pltpu.SemaphoreType.DMA((2, nazi)),
            pltpu.SemaphoreType.DMA((2, nazi)),
        ],
        compiler_params=pltpu.CompilerParams(
            collective_id=0, has_side_effects=True, vmem_limit_bytes=20 * 2**20
        ),
    )(pltpu.with_memory_space_constraint(x, pltpu.HBM))


def tiles_for(first, last):
    starts = list(range(first, last - 6, 8))
    if starts[-1] + 7 < last:
        starts.append(last - 7)
    return starts


def stage(src, base, dst, coef, tiles, old, new):
    nazi = src.shape[0]
    lane = lax.broadcasted_iota(jnp.int32, (8, LANES), 1)
    at_end, at_start = lane == LANES - 1, lane == 0

    def body(j, carry):
        before = lax.rem(j + nazi - 1, nazi)
        after = lax.rem(j + 1, nazi)
        for s in tiles:
            c0, d, ga, gb, h, s2, s5 = (coef[i, s : s + 8, :] for i in range(7))
            stiff = [coef[7 + k, s : s + 8, :] for k in range(LEVELS)]

            def cell(f, k):
                return src[j, f * LEVELS + k, s : s + 8, :]

            def around(f, k):
                p = f * LEVELS + k
                c = src[j, p, s : s + 8, :]
                up, lo = src[j, p, s + 1 : s + 9, :], src[j, p, s - 1 : s + 7, :]
                be = pltpu.roll(jnp.where(at_end, src[before, p, s : s + 8, :], c), 1, 1)
                ah = pltpu.roll(jnp.where(at_start, src[after, p, s : s + 8, :], c), LANES - 1, 1)
                return c, up, lo, ah, be

            def rest(parts):
                c, up, lo, ah, be = parts
                return c0 * c + d * (up + lo) + (ga * ah + gb * be)

            def vertical(f, k):
                if k == 0:
                    return cell(f, 1)
                if k == LEVELS - 1:
                    return -cell(f, k - 1)
                return cell(f, k + 1) - cell(f, k - 1)

            done = {}
            for k in range(LEVELS):
                rho, u, v, w, p = (around(f, k) for f in range(5))
                div = (u[1] - u[2]) + (v[3] - v[4]) + vertical(3, k)
                results = (
                    rest(rho) - h * div,
                    rest(u) + s2 * v[0] - h * (p[1] - p[2]),
                    rest(v) - s5 * u[0] - h * (p[3] - p[4]),
                    rest(w) - h * vertical(4, k),
                    rest(p) - stiff[k] * div,
                )
                for f, result in enumerate(results):
                    plane = f * LEVELS + k
                    if base is not None:
                        result = old * base[j, plane, s : s + 8, :] + new * result
                    done[plane] = result
            for plane, result in done.items():
                dst[j, plane, s : s + 8, :] = result
        return carry

    lax.fori_loop(0, nazi, body, 0, unroll=2)


def fill_coefficients(coef, first, shift_ref, spin_ref, drift_ref, stiff_ref):
    count = coef.shape[1] - 2 * HALO
    shape = (count, spin_ref.shape[1])
    radius = lax.broadcasted_iota(jnp.int32, shape, 0) + first
    match = radius == lax.broadcasted_iota(jnp.int32, shape, 1)

    def column(values):
        picked = jnp.sum(jnp.where(match, values, 0.0), axis=1, keepdims=True)
        return jnp.broadcast_to(picked, (count, LANES))

    c = time_step * diffuse
    half = 0.5 * time_step
    inside = column(jnp.ones((1, shape[1]), jnp.float32))
    spin, drift = column(spin_ref[...]), column(drift_ref[...])
    values = [
        (1.0 - 4.0 * c) * inside,
        c * inside,
        c * inside - half * drift,
        c * inside + half * drift,
        half * inside,
        2.0 * time_step * spin,
        half * spin,
    ]
    values += [half * column(stiff_ref[k : k + 1, :]) for k in range(LEVELS)]
    values.append(column(shift_ref[...].astype(jnp.float32)))
    for i, value in enumerate(values):
        coef[i, HALO : HALO + count, :] = value


def compute_kernel(shift_ref, spin_ref, drift_ref, stiff_ref, ext_ref, out_ref, coef_ref, one, two, three):
    nazi, planes, rows, cells = ext_ref.shape
    own_rows = rows - 2 * OWN
    rad, azi = lax.axis_index("rad"), lax.axis_index("azi")
    lane = lax.broadcasted_iota(jnp.int32, (8, LANES), 1)

    def rows_with(margin):
        return tiles_for(OWN - margin, rows - OWN - 1 + margin)

    group = max(1, planes * 4 // max(nazi, 4))
    fill_coefficients(coef_ref, rad * own_rows - HALO, shift_ref, spin_ref, drift_ref, stiff_ref)

    def amounts(s):
        shift = coef_ref[11, s : s + 8, :].astype(jnp.int32)
        return shift // LANES, shift % LANES

    def rotate(here, behind, offsets):
        mixed = jnp.where(lane >= LANES - offsets, behind, here)
        return jnp.take_along_axis(mixed, lax.rem(lane - offsets + LANES, LANES), axis=1)

    stage(ext_ref, None, one, coef_ref, rows_with(5), 0.0, 1.0)
    stage(one, ext_ref, two, coef_ref, rows_with(4), 0.75, 0.25)
    stage(two, ext_ref, three, coef_ref, rows_with(3), 1.0 / 3.0, 2.0 / 3.0)
    for s in rows_with(3):
        hops, offsets = amounts(s)

        def shifted(p, carry):
            blocks = [three[b, p, s : s + 8, :] for b in range(nazi)]
            blocks = [rotate(blocks[b], blocks[b - 1], offsets) for b in range(nazi)]
            for bit in range(nazi.bit_length() - 1):
                taken = (hops // (1 << bit)) % 2 == 1
                blocks = [jnp.where(taken, blocks[b - (1 << bit)], blocks[b]) for b in range(nazi)]
            for b in range(nazi):
                one[b, p, s : s + 8, :] = blocks[b]
            return carry

        lax.fori_loop(0, planes, shifted, 0, unroll=group)

    stage(one, None, two, coef_ref, rows_with(2), 0.0, 1.0)
    stage(two, one, three, coef_ref, rows_with(1), 0.75, 0.25)
    stage(three, one, two, coef_ref, rows_with(0), 1.0 / 3.0, 2.0 / 3.0)
    for s in rows_with(0):
        hops, offsets = amounts(s)
        source = lax.rem(azi - hops + nazi, nazi)

        def final(p, carry):
            blocks = [two[b, p, s : s + 8, :] for b in range(nazi)]
            here, behind = blocks[0], blocks[-1]
            for b in range(1, nazi):
                here = jnp.where(source == b, blocks[b], here)
                behind = jnp.where(source == b, blocks[b - 1], behind)
            out_ref[p, s - OWN : s - OWN + 8, :] = rotate(here, behind, offsets)
            return carry

        lax.fori_loop(0, planes, final, 0, unroll=group)


def on_device(state, shifts, spin, drift, stiffness):
    fields, levels, rows, cells = state.shape
    planes = fields * levels
    nrad, nazi = lax.axis_size("rad"), lax.axis_size("azi")
    flat = state.reshape(planes, rows, cells)
    ext = gathered(flat, nrad, nazi)
    whole = pltpu.VMEM(ext.shape, jnp.float32)
    out = pl.pallas_call(
        compute_kernel,
        out_shape=jax.ShapeDtypeStruct(flat.shape, jnp.float32),
        in_specs=[pl.BlockSpec(memory_space=pltpu.VMEM)] * 5,
        out_specs=pl.BlockSpec(memory_space=pltpu.VMEM),
        scratch_shapes=[pltpu.VMEM((12, rows + 2 * OWN, LANES), jnp.float32), whole, whole, whole],
        compiler_params=pltpu.CompilerParams(vmem_limit_bytes=40 * 2**20),
    )(shifts[None], spin[None], drift[None], stiffness, ext)
    return out.reshape(state.shape)


def solution(mesh):
    in_specs = (P(None, None, "rad", "azi"), P(), P(), P(), P())
    out_specs = P(None, None, "rad", "azi")
    return jax.shard_map(
        on_device, mesh=mesh, in_specs=in_specs, out_specs=out_specs, check_vma=False
    )
```

```python
import functools

import jax
import jax.numpy as jnp
from jax import lax
from jax.experimental import pallas as pl
from jax.experimental.pallas import tpu as pltpu
from jax.sharding import PartitionSpec as P

MESH = pl.DeviceIdType.MESH
STEPS = 2
HALO = 8
OWN = 16
LANES = 128
LEVELS = 4
time_step = 0.15
diffuse = 0.05


def gather_kernel(nrad, nazi, x_ref, ext_ref, zeros, own_sem, z_send, z_recv, h_send, h_recv, edge_sem, ready):
    rad, azi = lax.axis_index("rad"), lax.axis_index("azi")
    rows = x_ref.shape[1]
    has_low, has_high = rad > 0, rad < nrad - 1

    has_left, has_right = azi > 0, azi < nazi - 1
    half = x_ref.shape[0] // 2
    everywhere = ((has_left, rad, azi - 1), (has_right, rad, azi + 1), (has_low, rad - 1, azi), (has_high, rad + 1, azi))

    barrier = pltpu.get_barrier_semaphore()
    expected = 0
    for i, (present, to_rad, to_azi) in enumerate(everywhere):
        if i == 0:
            expected = expected + present.astype(jnp.int32)
            continue
        if i > 1:
            expected = expected + present.astype(jnp.int32)

        @pl.when(present)
        def _():
            pl.semaphore_signal(barrier, inc=1, device_id=(to_rad, to_azi), device_id_type=MESH)

    own = pltpu.make_async_copy(x_ref, ext_ref.at[azi, :, pl.ds(OWN, rows)], own_sem)
    own.start()
    zeros[...] = jnp.zeros_like(zeros)
    pl.semaphore_wait(barrier, expected)

    @pl.when(has_left)
    def _():
        pl.semaphore_signal(ready, inc=1, device_id=(rad, azi - 1), device_id_type=MESH)

    def planes(c):
        return pl.ds(c * half, half)

    def z_copy(side, t, c, block, src):
        return pltpu.make_async_remote_copy(
            src_ref=src,
            dst_ref=ext_ref.at[block, planes(c), pl.ds(OWN, rows)],
            send_sem=z_send.at[side, t, c],
            recv_sem=z_recv.at[side, t, c],
            device_id=(rad, azi + 1 if side == 0 else azi - 1),
            device_id_type=MESH,
        )

    def along(side, t, c):
        block = azi - t if side == 0 else azi + t
        src = x_ref.at[planes(c)] if t == 0 else ext_ref.at[block, planes(c), pl.ds(OWN, rows)]
        return z_copy(side, t, c, block, src)

    def sends(side, t):
        if side == 0:
            return jnp.logical_and(azi - t >= 0, has_right)
        return jnp.logical_and(azi + t < nazi, has_left)

    def came(side, t):
        return azi - 1 - t if side == 0 else azi + 1 + t

    def arrives(side, t):
        return came(side, t) >= 0 if side == 0 else came(side, t) < nazi

    def arrived(side, t, c):
        return z_copy(side, t, c, came(side, t), x_ref.at[planes(c)])

    def radial(to, block, c, own_block):
        if to == 0:
            start, there = 0, OWN + rows
        else:
            start, there = rows - HALO, OWN - HALO
        if own_block:
            src = x_ref.at[planes(c), pl.ds(start, HALO)]
        else:
            src = ext_ref.at[block, planes(c), pl.ds(OWN + start, HALO)]
        return pltpu.make_async_remote_copy(
            src_ref=src,
            dst_ref=ext_ref.at[block, planes(c), pl.ds(there, HALO)],
            send_sem=h_send.at[to, block, c],
            recv_sem=h_recv.at[to, block, c],
            device_id=(rad - 1 if to == 0 else rad + 1, azi),
            device_id_type=MESH,
        )

    def pass_on(block, c, own_block=False):
        @pl.when(has_low)
        def _():
            radial(0, block, c, own_block).start()

        @pl.when(has_high)
        def _():
            radial(1, block, c, own_block).start()

    def edge(b, side):
        start = OWN - HALO if side == 0 else OWN + rows
        return pltpu.make_async_copy(zeros, ext_ref.at[b, :, pl.ds(start, HALO)], edge_sem.at[side, b])

    @pl.when(has_left)
    def _():
        for c in range(2):
            along(1, 0, c).start()

    for c in range(2):
        pass_on(azi, c, True)

    @pl.when(has_right)
    def _():
        pl.semaphore_wait(ready, 1)
        for c in range(2):
            along(0, 0, c).start()

    for side, missing in enumerate((has_low, has_high)):

        @pl.when(jnp.logical_not(missing))
        def _():
            for b in range(nazi):
                edge(b, side).start()

    for t in range(nazi - 1):
        for c, side in ((0, 0), (0, 1), (1, 0), (1, 1)):

            @pl.when(arrives(side, t))
            def _():
                arrived(side, t, c).wait_recv()

                @pl.when(sends(side, t + 1))
                def _():
                    along(side, t + 1, c).start()

                pass_on(came(side, t), c)

    for side, missing in enumerate((has_low, has_high)):

        @pl.when(jnp.logical_not(missing))
        def _():
            for b in range(nazi):
                edge(b, side).wait()

    own.wait()
    for t in range(nazi - 1):
        for side in range(2):

            @pl.when(sends(side, t))
            def _():
                for c in range(2):
                    along(side, t, c).wait_send()

    @pl.when(has_low)
    def _():
        for b in range(nazi):
            for c in range(2):
                radial(0, b, c, False).wait_send()
                radial(1, b, c, False).wait_recv()

    @pl.when(has_high)
    def _():
        for b in range(nazi):
            for c in range(2):
                radial(1, b, c, False).wait_send()
                radial(0, b, c, False).wait_recv()


def gathered(x, nrad, nazi):
    planes, rows, cells = x.shape
    return pl.pallas_call(
        functools.partial(gather_kernel, nrad, nazi),
        out_shape=jax.ShapeDtypeStruct((nazi, planes, rows + 2 * OWN, cells), jnp.float32),
        in_specs=[pl.BlockSpec(memory_space=pltpu.HBM)],
        out_specs=pl.BlockSpec(memory_space=pltpu.VMEM),
        scratch_shapes=[
            pltpu.VMEM((planes, HALO, cells), jnp.float32),
            pltpu.SemaphoreType.DMA,
            pltpu.SemaphoreType.DMA((2, nazi, 2)),
            pltpu.SemaphoreType.DMA((2, nazi, 2)),
            pltpu.SemaphoreType.DMA((2, nazi, 2)),
            pltpu.SemaphoreType.DMA((2, nazi, 2)),
            pltpu.SemaphoreType.DMA((2, nazi)),
            pltpu.SemaphoreType.REGULAR,
        ],
        compiler_params=pltpu.CompilerParams(
            collective_id=0, has_side_effects=True, vmem_limit_bytes=20 * 2**20
        ),
    )(pltpu.with_memory_space_constraint(x, pltpu.HBM))


def tiles_for(first, last):
    starts = list(range(first, last - 6, 8))
    if starts[-1] + 7 < last:
        starts.append(last - 7)
    return starts


def stage(src, base, dst, coef, tiles, old, new):
    nazi = src.shape[0]
    lane = lax.broadcasted_iota(jnp.int32, (8, LANES), 1)
    at_end, at_start = lane == LANES - 1, lane == 0

    def body(j, carry):
        before = lax.rem(j + nazi - 1, nazi)
        after = lax.rem(j + 1, nazi)
        for s in tiles:
            c0, d, ga, gb, h, s2, s5 = (coef[i, s : s + 8, :] for i in range(7))
            stiff = [coef[7 + k, s : s + 8, :] for k in range(LEVELS)]

            def cell(f, k):
                return src[j, f * LEVELS + k, s : s + 8, :]

            def around(f, k):
                p = f * LEVELS + k
                c = src[j, p, s : s + 8, :]
                up, lo = src[j, p, s + 1 : s + 9, :], src[j, p, s - 1 : s + 7, :]
                be = pltpu.roll(jnp.where(at_end, src[before, p, s : s + 8, :], c), 1, 1)
                ah = pltpu.roll(jnp.where(at_start, src[after, p, s : s + 8, :], c), LANES - 1, 1)
                return c, up, lo, ah, be

            def rest(parts):
                c, up, lo, ah, be = parts
                return c0 * c + d * (up + lo) + (ga * ah + gb * be)

            def vertical(f, k):
                if k == 0:
                    return cell(f, 1)
                if k == LEVELS - 1:
                    return -cell(f, k - 1)
                return cell(f, k + 1) - cell(f, k - 1)

            done = {}
            for k in range(LEVELS):
                rho, u, v, w, p = (around(f, k) for f in range(5))
                div = (u[1] - u[2]) + (v[3] - v[4]) + vertical(3, k)
                results = (
                    rest(rho) - h * div,
                    rest(u) + s2 * v[0] - h * (p[1] - p[2]),
                    rest(v) - s5 * u[0] - h * (p[3] - p[4]),
                    rest(w) - h * vertical(4, k),
                    rest(p) - stiff[k] * div,
                )
                for f, result in enumerate(results):
                    plane = f * LEVELS + k
                    if base is not None:
                        result = old * base[j, plane, s : s + 8, :] + new * result
                    done[plane] = result
            for plane, result in done.items():
                dst[j, plane, s : s + 8, :] = result
        return carry

    lax.fori_loop(0, nazi, body, 0, unroll=4)


def fill_coefficients(coef, first, shift_ref, spin_ref, drift_ref, stiff_ref):
    count = coef.shape[1] - 2 * HALO
    shape = (count, spin_ref.shape[1])
    radius = lax.broadcasted_iota(jnp.int32, shape, 0) + first
    match = radius == lax.broadcasted_iota(jnp.int32, shape, 1)

    def column(values):
        picked = jnp.sum(jnp.where(match, values, 0.0), axis=1, keepdims=True)
        return jnp.broadcast_to(picked, (count, LANES))

    c = time_step * diffuse
    half = 0.5 * time_step
    inside = column(jnp.ones((1, shape[1]), jnp.float32))
    spin, drift = column(spin_ref[...]), column(drift_ref[...])
    values = [
        (1.0 - 4.0 * c) * inside,
        c * inside,
        c * inside - half * drift,
        c * inside + half * drift,
        half * inside,
        2.0 * time_step * spin,
        half * spin,
    ]
    values += [half * column(stiff_ref[k : k + 1, :]) for k in range(LEVELS)]
    values.append(column(shift_ref[...].astype(jnp.float32)))
    for i, value in enumerate(values):
        coef[i, HALO : HALO + count, :] = value


def compute_kernel(shift_ref, spin_ref, drift_ref, stiff_ref, ext_ref, out_ref, coef_ref, one, two, three):
    nazi, planes, rows, cells = ext_ref.shape
    own_rows = rows - 2 * OWN
    rad, azi = lax.axis_index("rad"), lax.axis_index("azi")
    lane = lax.broadcasted_iota(jnp.int32, (8, LANES), 1)

    def rows_with(margin):
        return tiles_for(OWN - margin, rows - OWN - 1 + margin)

    group = max(1, planes * 4 // max(nazi, 4))
    fill_coefficients(coef_ref, rad * own_rows - HALO, shift_ref, spin_ref, drift_ref, stiff_ref)

    def amounts(s):
        shift = coef_ref[11, s : s + 8, :].astype(jnp.int32)
        return shift // LANES, shift % LANES

    def rotate(here, behind, offsets):
        mixed = jnp.where(lane >= LANES - offsets, behind, here)
        return jnp.take_along_axis(mixed, lax.rem(lane - offsets + LANES, LANES), axis=1)

    stage(ext_ref, None, one, coef_ref, rows_with(5), 0.0, 1.0)
    stage(one, ext_ref, two, coef_ref, rows_with(4), 0.75, 0.25)
    stage(two, ext_ref, three, coef_ref, rows_with(3), 1.0 / 3.0, 2.0 / 3.0)
    for s in rows_with(3):
        hops, offsets = amounts(s)

        def shifted(p, carry):
            blocks = [three[b, p, s : s + 8, :] for b in range(nazi)]
            blocks = [rotate(blocks[b], blocks[b - 1], offsets) for b in range(nazi)]
            for bit in range(nazi.bit_length() - 1):
                taken = (hops // (1 << bit)) % 2 == 1
                blocks = [jnp.where(taken, blocks[b - (1 << bit)], blocks[b]) for b in range(nazi)]
            for b in range(nazi):
                one[b, p, s : s + 8, :] = blocks[b]
            return carry

        lax.fori_loop(0, planes, shifted, 0, unroll=group)

    stage(one, None, two, coef_ref, rows_with(2), 0.0, 1.0)
    stage(two, one, three, coef_ref, rows_with(1), 0.75, 0.25)
    stage(three, one, two, coef_ref, rows_with(0), 1.0 / 3.0, 2.0 / 3.0)
    for s in rows_with(0):
        hops, offsets = amounts(s)
        source = lax.rem(azi - hops + nazi, nazi)

        def final(p, carry):
            blocks = [two[b, p, s : s + 8, :] for b in range(nazi)]
            here, behind = blocks[0], blocks[-1]
            for b in range(1, nazi):
                here = jnp.where(source == b, blocks[b], here)
                behind = jnp.where(source == b, blocks[b - 1], behind)
            out_ref[p, s - OWN : s - OWN + 8, :] = rotate(here, behind, offsets)
            return carry

        lax.fori_loop(0, planes, final, 0, unroll=group)


def on_device(state, shifts, spin, drift, stiffness):
    fields, levels, rows, cells = state.shape
    planes = fields * levels
    nrad, nazi = lax.axis_size("rad"), lax.axis_size("azi")
    flat = state.reshape(planes, rows, cells)
    ext = gathered(flat, nrad, nazi)
    whole = pltpu.VMEM(ext.shape, jnp.float32)
    out = pl.pallas_call(
        compute_kernel,
        out_shape=jax.ShapeDtypeStruct(flat.shape, jnp.float32),
        in_specs=[pl.BlockSpec(memory_space=pltpu.VMEM)] * 5,
        out_specs=pl.BlockSpec(memory_space=pltpu.VMEM),
        scratch_shapes=[pltpu.VMEM((12, rows + 2 * OWN, LANES), jnp.float32), whole, whole, whole],
        compiler_params=pltpu.CompilerParams(vmem_limit_bytes=40 * 2**20),
    )(shifts[None], spin[None], drift[None], stiffness, ext)
    return out.reshape(state.shape)


def solution(mesh):
    in_specs = (P(None, None, "rad", "azi"), P(), P(), P(), P())
    out_specs = P(None, None, "rad", "azi")
    return jax.shard_map(
        on_device, mesh=mesh, in_specs=in_specs, out_specs=out_specs, check_vma=False
    )
```

```python
import functools

import jax
import jax.numpy as jnp
from jax import lax
from jax.experimental import pallas as pl
from jax.experimental.pallas import tpu as pltpu
from jax.sharding import PartitionSpec as P

MESH = pl.DeviceIdType.MESH
STEPS = 2
HALO = 8
OWN = 16
LANES = 128
LEVELS = 4
PARTS = 4
time_step = 0.15
diffuse = 0.05


def gather_kernel(nrad, nazi, x_ref, ext_ref, zeros, own_sem, z_send, z_recv, h_send, h_recv, edge_sem, ready):
    rad, azi = lax.axis_index("rad"), lax.axis_index("azi")
    rows = x_ref.shape[1]
    has_low, has_high = rad > 0, rad < nrad - 1

    has_left, has_right = azi > 0, azi < nazi - 1
    part = x_ref.shape[0] // PARTS
    everywhere = ((has_left, rad, azi - 1), (has_right, rad, azi + 1), (has_low, rad - 1, azi), (has_high, rad + 1, azi))

    barrier = pltpu.get_barrier_semaphore()
    expected = 0
    for i, (present, to_rad, to_azi) in enumerate(everywhere):
        if i == 0:
            expected = expected + present.astype(jnp.int32)
            continue
        if i > 1:
            expected = expected + present.astype(jnp.int32)

        @pl.when(present)
        def _():
            pl.semaphore_signal(barrier, inc=1, device_id=(to_rad, to_azi), device_id_type=MESH)

    own = pltpu.make_async_copy(x_ref, ext_ref.at[azi, :, pl.ds(OWN, rows)], own_sem)
    own.start()
    zeros[...] = jnp.zeros_like(zeros)
    pl.semaphore_wait(barrier, expected)

    @pl.when(has_left)
    def _():
        pl.semaphore_signal(ready, inc=1, device_id=(rad, azi - 1), device_id_type=MESH)

    def planes(c):
        return pl.ds(c * part, part)

    def z_copy(side, t, c, block, src):
        return pltpu.make_async_remote_copy(
            src_ref=src,
            dst_ref=ext_ref.at[block, planes(c), pl.ds(OWN, rows)],
            send_sem=z_send.at[side, t, c],
            recv_sem=z_recv.at[side, t, c],
            device_id=(rad, azi + 1 if side == 0 else azi - 1),
            device_id_type=MESH,
        )

    def along(side, t, c):
        block = azi - t if side == 0 else azi + t
        src = x_ref.at[planes(c)] if t == 0 else ext_ref.at[block, planes(c), pl.ds(OWN, rows)]
        return z_copy(side, t, c, block, src)

    def sends(side, t):
        if side == 0:
            return jnp.logical_and(azi - t >= 0, has_right)
        return jnp.logical_and(azi + t < nazi, has_left)

    def came(side, t):
        return azi - 1 - t if side == 0 else azi + 1 + t

    def arrives(side, t):
        return came(side, t) >= 0 if side == 0 else came(side, t) < nazi

    def arrived(side, t, c):
        return z_copy(side, t, c, came(side, t), x_ref.at[planes(c)])

    def radial(to, block, c, own_block):
        if to == 0:
            start, there = 0, OWN + rows
        else:
            start, there = rows - HALO, OWN - HALO
        if own_block:
            src = x_ref.at[planes(c), pl.ds(start, HALO)]
        else:
            src = ext_ref.at[block, planes(c), pl.ds(OWN + start, HALO)]
        return pltpu.make_async_remote_copy(
            src_ref=src,
            dst_ref=ext_ref.at[block, planes(c), pl.ds(there, HALO)],
            send_sem=h_send.at[to, block, c],
            recv_sem=h_recv.at[to, block, c],
            device_id=(rad - 1 if to == 0 else rad + 1, azi),
            device_id_type=MESH,
        )

    def pass_on(block, c, own_block=False):
        @pl.when(has_low)
        def _():
            radial(0, block, c, own_block).start()

        @pl.when(has_high)
        def _():
            radial(1, block, c, own_block).start()

    def edge(b, side):
        start = OWN - HALO if side == 0 else OWN + rows
        return pltpu.make_async_copy(zeros, ext_ref.at[b, :, pl.ds(start, HALO)], edge_sem.at[side, b])

    @pl.when(has_left)
    def _():
        for c in range(PARTS):
            along(1, 0, c).start()

    for c in range(PARTS):
        pass_on(azi, c, True)

    @pl.when(has_right)
    def _():
        pl.semaphore_wait(ready, 1)
        for c in range(PARTS):
            along(0, 0, c).start()

    for side, missing in enumerate((has_low, has_high)):

        @pl.when(jnp.logical_not(missing))
        def _():
            for b in range(nazi):
                edge(b, side).start()

    for t in range(nazi - 1):
        for c, side in [(c, side) for c in range(PARTS) for side in range(2)]:

            @pl.when(arrives(side, t))
            def _():
                arrived(side, t, c).wait_recv()

                @pl.when(sends(side, t + 1))
                def _():
                    along(side, t + 1, c).start()

                pass_on(came(side, t), c)

    for side, missing in enumerate((has_low, has_high)):

        @pl.when(jnp.logical_not(missing))
        def _():
            for b in range(nazi):
                edge(b, side).wait()

    own.wait()
    for t in range(nazi - 1):
        for side in range(2):

            @pl.when(sends(side, t))
            def _():
                for c in range(PARTS):
                    along(side, t, c).wait_send()

    @pl.when(has_low)
    def _():
        for b in range(nazi):
            for c in range(PARTS):
                radial(0, b, c, False).wait_send()
                radial(1, b, c, False).wait_recv()

    @pl.when(has_high)
    def _():
        for b in range(nazi):
            for c in range(PARTS):
                radial(1, b, c, False).wait_send()
                radial(0, b, c, False).wait_recv()


def gathered(x, nrad, nazi):
    planes, rows, cells = x.shape
    return pl.pallas_call(
        functools.partial(gather_kernel, nrad, nazi),
        out_shape=jax.ShapeDtypeStruct((nazi, planes, rows + 2 * OWN, cells), jnp.float32),
        in_specs=[pl.BlockSpec(memory_space=pltpu.HBM)],
        out_specs=pl.BlockSpec(memory_space=pltpu.VMEM),
        scratch_shapes=[
            pltpu.VMEM((planes, HALO, cells), jnp.float32),
            pltpu.SemaphoreType.DMA,
            pltpu.SemaphoreType.DMA((2, nazi, PARTS)),
            pltpu.SemaphoreType.DMA((2, nazi, PARTS)),
            pltpu.SemaphoreType.DMA((2, nazi, PARTS)),
            pltpu.SemaphoreType.DMA((2, nazi, PARTS)),
            pltpu.SemaphoreType.DMA((2, nazi)),
            pltpu.SemaphoreType.REGULAR,
        ],
        compiler_params=pltpu.CompilerParams(
            collective_id=0, has_side_effects=True, vmem_limit_bytes=20 * 2**20
        ),
    )(pltpu.with_memory_space_constraint(x, pltpu.HBM))


def tiles_for(first, last):
    starts = list(range(first, last - 6, 8))
    if starts[-1] + 7 < last:
        starts.append(last - 7)
    return starts


def stage(src, base, dst, coef, tiles, old, new):
    nazi = src.shape[0]
    lane = lax.broadcasted_iota(jnp.int32, (8, LANES), 1)
    at_end, at_start = lane == LANES - 1, lane == 0

    def body(j, carry):
        before = lax.rem(j + nazi - 1, nazi)
        after = lax.rem(j + 1, nazi)
        for s in tiles:
            c0, d, ga, gb, h, s2, s5 = (coef[i, s : s + 8, :] for i in range(7))
            stiff = [coef[7 + k, s : s + 8, :] for k in range(LEVELS)]

            def cell(f, k):
                return src[j, f * LEVELS + k, s : s + 8, :]

            def around(f, k):
                p = f * LEVELS + k
                c = src[j, p, s : s + 8, :]
                up, lo = src[j, p, s + 1 : s + 9, :], src[j, p, s - 1 : s + 7, :]
                be = pltpu.roll(jnp.where(at_end, src[before, p, s : s + 8, :], c), 1, 1)
                ah = pltpu.roll(jnp.where(at_start, src[after, p, s : s + 8, :], c), LANES - 1, 1)
                return c, up, lo, ah, be

            def rest(parts):
                c, up, lo, ah, be = parts
                return c0 * c + d * (up + lo) + (ga * ah + gb * be)

            def vertical(f, k):
                if k == 0:
                    return cell(f, 1)
                if k == LEVELS - 1:
                    return -cell(f, k - 1)
                return cell(f, k + 1) - cell(f, k - 1)

            done = {}
            for k in range(LEVELS):
                rho, u, v, w, p = (around(f, k) for f in range(5))
                div = (u[1] - u[2]) + (v[3] - v[4]) + vertical(3, k)
                results = (
                    rest(rho) - h * div,
                    rest(u) + s2 * v[0] - h * (p[1] - p[2]),
                    rest(v) - s5 * u[0] - h * (p[3] - p[4]),
                    rest(w) - h * vertical(4, k),
                    rest(p) - stiff[k] * div,
                )
                for f, result in enumerate(results):
                    plane = f * LEVELS + k
                    if base is not None:
                        result = old * base[j, plane, s : s + 8, :] + new * result
                    done[plane] = result
            for plane, result in done.items():
                dst[j, plane, s : s + 8, :] = result
        return carry

    lax.fori_loop(0, nazi, body, 0, unroll=2)


def fill_coefficients(coef, first, shift_ref, spin_ref, drift_ref, stiff_ref):
    count = coef.shape[1] - 2 * HALO
    shape = (count, spin_ref.shape[1])
    radius = lax.broadcasted_iota(jnp.int32, shape, 0) + first
    match = radius == lax.broadcasted_iota(jnp.int32, shape, 1)

    def column(values):
        picked = jnp.sum(jnp.where(match, values, 0.0), axis=1, keepdims=True)
        return jnp.broadcast_to(picked, (count, LANES))

    c = time_step * diffuse
    half = 0.5 * time_step
    inside = column(jnp.ones((1, shape[1]), jnp.float32))
    spin, drift = column(spin_ref[...]), column(drift_ref[...])
    values = [
        (1.0 - 4.0 * c) * inside,
        c * inside,
        c * inside - half * drift,
        c * inside + half * drift,
        half * inside,
        2.0 * time_step * spin,
        half * spin,
    ]
    values += [half * column(stiff_ref[k : k + 1, :]) for k in range(LEVELS)]
    values.append(column(shift_ref[...].astype(jnp.float32)))
    for i, value in enumerate(values):
        coef[i, HALO : HALO + count, :] = value


def compute_kernel(shift_ref, spin_ref, drift_ref, stiff_ref, ext_ref, out_ref, coef_ref, one, two, three):
    nazi, planes, rows, cells = ext_ref.shape
    own_rows = rows - 2 * OWN
    rad, azi = lax.axis_index("rad"), lax.axis_index("azi")
    lane = lax.broadcasted_iota(jnp.int32, (8, LANES), 1)

    def rows_with(margin):
        return tiles_for(OWN - margin, rows - OWN - 1 + margin)

    group = max(1, planes * 4 // max(nazi, 4))
    fill_coefficients(coef_ref, rad * own_rows - HALO, shift_ref, spin_ref, drift_ref, stiff_ref)

    def amounts(s):
        shift = coef_ref[11, s : s + 8, :].astype(jnp.int32)
        return shift // LANES, shift % LANES

    def rotate(here, behind, offsets):
        mixed = jnp.where(lane >= LANES - offsets, behind, here)
        return jnp.take_along_axis(mixed, lax.rem(lane - offsets + LANES, LANES), axis=1)

    stage(ext_ref, None, one, coef_ref, rows_with(5), 0.0, 1.0)
    stage(one, ext_ref, two, coef_ref, rows_with(4), 0.75, 0.25)
    stage(two, ext_ref, three, coef_ref, rows_with(3), 1.0 / 3.0, 2.0 / 3.0)
    for s in rows_with(3):
        hops, offsets = amounts(s)

        def shifted(p, carry):
            blocks = [three[b, p, s : s + 8, :] for b in range(nazi)]
            blocks = [rotate(blocks[b], blocks[b - 1], offsets) for b in range(nazi)]
            for bit in range(nazi.bit_length() - 1):
                taken = (hops // (1 << bit)) % 2 == 1
                blocks = [jnp.where(taken, blocks[b - (1 << bit)], blocks[b]) for b in range(nazi)]
            for b in range(nazi):
                one[b, p, s : s + 8, :] = blocks[b]
            return carry

        lax.fori_loop(0, planes, shifted, 0, unroll=group)

    stage(one, None, two, coef_ref, rows_with(2), 0.0, 1.0)
    stage(two, one, three, coef_ref, rows_with(1), 0.75, 0.25)
    stage(three, one, two, coef_ref, rows_with(0), 1.0 / 3.0, 2.0 / 3.0)
    for s in rows_with(0):
        hops, offsets = amounts(s)
        source = lax.rem(azi - hops + nazi, nazi)

        def final(p, carry):
            blocks = [two[b, p, s : s + 8, :] for b in range(nazi)]
            here, behind = blocks[0], blocks[-1]
            for b in range(1, nazi):
                here = jnp.where(source == b, blocks[b], here)
                behind = jnp.where(source == b, blocks[b - 1], behind)
            out_ref[p, s - OWN : s - OWN + 8, :] = rotate(here, behind, offsets)
            return carry

        lax.fori_loop(0, planes, final, 0, unroll=group)


def on_device(state, shifts, spin, drift, stiffness):
    fields, levels, rows, cells = state.shape
    planes = fields * levels
    nrad, nazi = lax.axis_size("rad"), lax.axis_size("azi")
    flat = state.reshape(planes, rows, cells)
    ext = gathered(flat, nrad, nazi)
    whole = pltpu.VMEM(ext.shape, jnp.float32)
    out = pl.pallas_call(
        compute_kernel,
        out_shape=jax.ShapeDtypeStruct(flat.shape, jnp.float32),
        in_specs=[pl.BlockSpec(memory_space=pltpu.VMEM)] * 5,
        out_specs=pl.BlockSpec(memory_space=pltpu.VMEM),
        scratch_shapes=[pltpu.VMEM((12, rows + 2 * OWN, LANES), jnp.float32), whole, whole, whole],
        compiler_params=pltpu.CompilerParams(vmem_limit_bytes=40 * 2**20),
    )(shifts[None], spin[None], drift[None], stiffness, ext)
    return out.reshape(state.shape)


def solution(mesh):
    in_specs = (P(None, None, "rad", "azi"), P(), P(), P(), P())
    out_specs = P(None, None, "rad", "azi")
    return jax.shard_map(
        on_device, mesh=mesh, in_specs=in_specs, out_specs=out_specs, check_vma=False
    )
```
